1024 devices in a mesh: grp: 2 (over y_lo), dp: 32 (over y_hi, z), blk: 16 (over x, core).
Axes of the slice: x: 8, y: 8 (y_hi: 4, y_lo: 2; y = y_hi * 2 + y_lo), z: 8, core: 2. Of those that a mesh axis runs over, the one named last changes fastest.
Arguments:
- layer_input: bfloat16 [64, 2048, 3584], P(('grp', 'dp'), 'blk'), may hold values from -16 to 16
- queries: bfloat16 [64, 2048, 1792], P(('grp', 'dp'), 'blk'), may hold values from -8 to 8
- keys: bfloat16 [64, 2048, 256], P(('grp', 'dp'), 'blk'), may hold values from -8 to 8
- d_out: bfloat16 [64, 2048, 1792], P(('grp', 'dp'), 'blk'), may hold values from -6 to 6
- doc_start: int32 [64, 2048], P(('grp', 'dp'), 'blk'), may hold values from 0 to 2047, as said below
- moment_m: float32 [3584, 256], P(('grp', 'dp'), 'blk'), may hold values from -0.3 to 0.3
- moment_v: float32 [3584, 256], P(('grp', 'dp'), 'blk'), may hold values from 0.001 to 0.01
Outputs:
- new_m: float32 [3584, 256], P(('grp', 'dp'), 'blk')
- new_v: float32 [3584, 256], P(('grp', 'dp'), 'blk')
- update: float32 [3584, 256], P(('grp', 'dp'), 'blk')
The draws below stay inside these ranges and needn't reach their ends.
Inputs may be any that keep to these rules, and one draw needn't show every extreme that they name: `doc_start`: the first 32 slots hold one document each; each other slot holds 16 sequences of 128 tokens, positions k * 128 to (k + 1) * 128 - 1, in which documents are consecutive runs of 1 to 64 tokens, the first exactly 64 long, the last a single token.
All inputs are finite; a program needn't handle non-finite values.
Results may differ from the reference program's by a relative error of at most 0.0071.
Values may be sent and summed in bfloat16 or wider, within the bound.
No kernel may reach another device: no remote copies, remote signals or barrier semaphores. Data moves between devices by JAX's collectives and lax.ppermute only.
A program may use at most 32 MiB of HBM per device.

```python
import math
import jax
import jax.numpy as jnp
from jax import lax

D = 3584
HEADS = 14
KV_HEADS = 2
HD = 128
STEP = 10
TOK_DEV = 128
GROUP = 7
TOKENS = 2048
SEQS = 64
DOC_MOST = 64
N_DP = 32
N_BLK = 16


def draw_queries(key, part):
    shape = (SEQS, TOKENS, HEADS * HD)
    values = jnp.clip(jax.random.normal(jax.random.fold_in(key, 1), shape, jnp.float32), -6.0, 6.0)
    return values.astype(jnp.bfloat16)


def draw_keys(key, part):
    shape = (SEQS, TOKENS, KV_HEADS * HD)
    values = jnp.clip(jax.random.normal(jax.random.fold_in(key, 2), shape, jnp.float32), -6.0, 6.0)
    return values.astype(jnp.bfloat16)


def draw_doc_start(key, part):
    lengths = jax.random.randint(jax.random.fold_in(key, 3), (SEQS * N_BLK, TOK_DEV), 1, DOC_MOST + 1)
    lengths = lengths.astype(jnp.int32).at[:, 0].set(DOC_MOST)
    ends = jnp.cumsum(lengths, axis=1).astype(jnp.int32)
    begins = (ends - lengths).astype(jnp.int32)
    positions = jnp.arange(TOK_DEV, dtype=jnp.int32)
    owner = jax.vmap(lambda row_ends: jnp.searchsorted(row_ends, positions, side='right'))(ends)
    starts = jnp.take_along_axis(begins, owner.astype(jnp.int32), axis=1).astype(jnp.int32)
    starts = starts.at[:, TOK_DEV - 1].set(TOK_DEV - 1)
    offsets = (jnp.arange(N_BLK, dtype=jnp.int32) * TOK_DEV)[None, :, None]
    starts = (starts.reshape(SEQS, N_BLK, TOK_DEV) + offsets).reshape(SEQS, TOKENS)
    sequence = jnp.arange(SEQS, dtype=jnp.int32)[:, None]
    return jnp.where(sequence < N_DP, 0, starts).astype(jnp.int32)


def raised(drawn, key, source, target, shards_of, factor):
    owner, partner = [(jnp.arange(drawn.shape[dim]) // (drawn.shape[dim] // shards_of)).reshape([-1 if axis == dim else 1 for axis in range(drawn.ndim)]) for dim in (source, target)]
    chosen = jax.random.permutation(key, shards_of)[partner]
    strong = (owner == chosen) | (owner == (partner + shards_of // 2) % shards_of)
    return jnp.where(strong, factor * drawn, drawn)


def block_scale(key, dims, shards, smallest, top_value):
    level, own = 1.0, jax.random.fold_in(key, 6)
    for axis_at, blocks in shards:
        draws = jnp.exp(jax.random.uniform(jax.random.fold_in(own, axis_at), (blocks,), jnp.float32, smallest / len(shards), top_value / len(shards)))
        level = level * jnp.repeat(draws, dims[axis_at] // blocks).reshape([-1 if axis == axis_at else 1 for axis in range(len(dims))])
    return level


def centred(rng, dims, scale, most, split=(), kind=jnp.bfloat16):
    gain = block_scale(rng, dims, split, -0.22, 0.18) if split else 1.0
    drawn = jax.random.normal(rng, dims, jnp.float32) * scale * gain
    return jnp.minimum(jnp.maximum(drawn, -most), most).astype(kind)


def gaussian_with(own_key, shape, width, reach, pieces, heavy, kind=jnp.bfloat16):
    result = width * jax.random.normal(own_key, shape, jnp.float32)
    if pieces:
        result = result * block_scale(own_key, shape, pieces, -0.22, 0.18)
    return jnp.clip(raised(result, jax.random.fold_in(own_key, 3), *heavy), -reach, reach).astype(kind)


def setup_inputs(seed: int = 0) -> dict:
    streams_of = jax.random.split(jax.random.key(seed), 8)
    return {
        "layer_input": gaussian_with(streams_of[0], (SEQS, TOKENS, D), 1.0, 16.0, ((0, 64), (1, 16)), (0, 2, 64, 4.0)),
        "queries": draw_queries(jax.random.fold_in(streams_of[7], 71), 0),
        "keys": draw_keys(jax.random.fold_in(streams_of[7], 71), 0),
        "d_out": centred(streams_of[3], (SEQS, TOKENS, HEADS * HD), 1.0, 6.0, ((0, 64), (1, 16))),
        "doc_start": draw_doc_start(jax.random.fold_in(streams_of[7], 71), 0),
        "moment_m": centred(streams_of[5], (D, KV_HEADS * HD), 0.05, 0.3, ((0, 64), (1, 16)), jnp.float32),
        "moment_v": jnp.clip(jnp.exp(math.log(0.01) - 2.30258502 * jax.random.uniform(streams_of[6], (D, KV_HEADS * HD), jnp.float32) ** block_scale(streams_of[6], (D, KV_HEADS * HD), ((0, 64), (1, 16)), -0.2, 0.2)), 0.001, 0.01),
    }


masked_score = -1e+30

def sequence_gradient(layer_rows, query_rows, key_rows, dout_rows, begin_rows):
    q_heads = query_rows.astype(jnp.float32).reshape(TOKENS, KV_HEADS, GROUP, HD)
    key_mat = key_rows.astype(jnp.float32).reshape(TOKENS, KV_HEADS, HD)
    d_heads = dout_rows.astype(jnp.float32).reshape(TOKENS, KV_HEADS, GROUP, HD)
    key_pos = jnp.arange(TOKENS, dtype=jnp.int32)
    block_rows = math.gcd(TOKENS, 512)

    def one_block(value_sum, block_index):
        first_row = (block_index * block_rows).astype(jnp.int32)
        q_block = lax.dynamic_slice_in_dim(q_heads, first_row, block_rows, 0)
        d_block = lax.dynamic_slice_in_dim(d_heads, first_row, block_rows, 0)
        begin = lax.dynamic_slice_in_dim(begin_rows, first_row, block_rows, 0)
        query_pos = first_row + jnp.arange(block_rows, dtype=jnp.int32)
        scores = jnp.einsum('rgph,kgh->gprk', q_block, key_mat) * HD ** (-0.5)
        visible = (key_pos[None, :] >= begin[:, None]) & (key_pos[None, :] <= query_pos[:, None])
        scores = jnp.where(visible, scores, masked_score)
        row_max = lax.optimization_barrier(jnp.max(scores, axis=-1, keepdims=True))
        summed = lax.optimization_barrier(jnp.sum(jnp.where(visible, jnp.exp(scores - row_max), 0.0), axis=-1, keepdims=True))
        log_total = row_max + jnp.log(summed)
        probs = jnp.where(visible, jnp.exp(jnp.where(visible, scores - log_total, masked_score)), 0.0)
        probs = lax.optimization_barrier(probs.astype(jnp.bfloat16)).astype(jnp.float32)
        value_sum = value_sum + jnp.einsum('gprk,rgph->kgh', probs, d_block)
        return (value_sum, None)
    value_sum, unused = lax.scan(one_block, jnp.zeros((TOKENS, KV_HEADS, HD), jnp.float32), jnp.arange(TOKENS // block_rows, dtype=jnp.int32))
    value_grad = value_sum.reshape(TOKENS, KV_HEADS * HD).astype(jnp.bfloat16)
    value_grad = lax.optimization_barrier(value_grad).astype(jnp.float32)
    return jnp.einsum('rd,rc->dc', layer_rows.astype(jnp.float32), value_grad)

def reference(layer_input, queries, keys, d_out, doc_start, moment_m, moment_v):

    def add_sequence(running, index):
        partial_value = sequence_gradient(layer_input[index], queries[index], keys[index], d_out[index], doc_start[index])
        return (running + partial_value, None)
    gradient, unused = lax.scan(add_sequence, jnp.zeros((D, KV_HEADS * HD), jnp.float32), jnp.arange(SEQS, dtype=jnp.int32))
    gradient = gradient * (1.0 / math.sqrt(SEQS * TOKENS))
    new_m = 0.9 * moment_m + 0.1 * gradient
    new_v = 0.95 * moment_v + 0.05 * gradient * gradient
    update = new_m / (1.0 - 0.9 ** STEP) / (jnp.sqrt(new_v / (1.0 - 0.95 ** STEP)) + 1e-08)
    return (new_m, new_v, update)
```

```python
import functools
import math

import jax
import jax.numpy as jnp
from jax import lax
from jax.experimental import pallas as pl
from jax.experimental.pallas import tpu as pltpu
from jax.sharding import PartitionSpec as P

KV_HEADS = 2
HD = 128
STEP = 10
GROUP = 7
CHUNK = 512
TILE = 512
masked_score = -1e30
WHOLE = pl.BlockSpec(memory_space=pltpu.VMEM)
SCALARS = pl.BlockSpec(memory_space=pltpu.SMEM)
PARAMS = pltpu.CompilerParams(vmem_limit_bytes=48 * 1024 * 1024)


def attention_kernel(place, begin, q, d, k0, k1, out, own, qs, ds, s):
    seq, rows_here = k0.shape[0], q.shape[0]
    width = GROUP * rows_here
    low, high, first_row = place[0], place[1], place[2]
    gain = HD ** (-0.5) * math.log2(math.e)
    for h in range(KV_HEADS * GROUP):
        g, r = divmod(h, GROUP)
        qs[g, r * rows_here : (r + 1) * rows_here, :] = q[:, h * HD : (h + 1) * HD]
        ds[g, r * rows_here : (r + 1) * rows_here, :] = d[:, h * HD : (h + 1) * HD]

    def chunk_rows(c):
        return pl.ds(pl.multiple_of(c * CHUNK, CHUNK), CHUNK)

    def clear(c, carry):
        @pl.when((c < low) | (c > high))
        def _():
            out[chunk_rows(c), :] = jnp.zeros((CHUNK, KV_HEADS * HD), out.dtype)

        return carry

    lax.fori_loop(0, seq // CHUNK, clear, 0)
    begin_all = jnp.concatenate([begin[...]] * GROUP, axis=1)
    query_pos = first_row + jnp.concatenate(
        [lax.broadcasted_iota(jnp.int32, (1, rows_here), 1)] * GROUP, axis=1
    )
    for g, k in enumerate((k0, k1)):
        cols = slice(g * HD, (g + 1) * HD)

        def scores(c):
            return gain * lax.dot_general(
                k[chunk_rows(c), :],
                qs[g],
                (((1,), (1,)), ((), ())),
                preferred_element_type=jnp.float32,
            )

        def larger(x, top):
            return jnp.maximum(top, jnp.max(x.reshape(CHUNK // 8, 8, width), axis=0))

        def inner(c, top):
            x = scores(c)
            s[chunk_rows(c), :] = x
            return larger(x, top)

        top = lax.fori_loop(low, high, inner, jnp.full((8, width), masked_score, jnp.float32))
        x = scores(high)
        key_pos = high * CHUNK + lax.broadcasted_iota(jnp.int32, (CHUNK, width), 0)
        x = jnp.where((key_pos >= begin_all) & (key_pos <= query_pos), x, masked_score)
        s[chunk_rows(high), :] = x
        top = jnp.max(larger(x, top), axis=0, keepdims=True)

        def weigh(c, total):
            p = jnp.exp2(s[chunk_rows(c), :] - top)
            return total + jnp.sum(p.reshape(CHUNK // 8, 8, width), axis=0)

        total = lax.fori_loop(low, high + 1, weigh, jnp.zeros((8, width), jnp.float32))
        shift = top + jnp.log2(jnp.sum(total, axis=0, keepdims=True))

        def collect(c):
            p = jnp.exp2(s[chunk_rows(c), :] - shift).astype(ds.dtype)
            block = jnp.dot(p, ds[g], preferred_element_type=jnp.float32)
            out[chunk_rows(c), cols] = block.astype(out.dtype)
            return block

        def inner_collect(c, carry):
            collect(c)
            return carry

        lax.fori_loop(low, high, inner_collect, 0)
        block = collect(high)
        for i in range(CHUNK // rows_here):

            @pl.when(first_row == high * CHUNK + i * rows_here)
            def _():
                own[:, cols] = block[i * rows_here : (i + 1) * rows_here]


def project_kernel(place, own, pieces, x, keep, send, vg):
    n, rows, cols = pieces.shape
    total = own[...]
    for i in range(n):
        total = total + jnp.where(place[1] == i, 0.0, pieces[i].astype(jnp.float32))
    vg[...] = jnp.transpose(total).astype(vg.dtype)

    def emit(even, odd):
        for t in range(x.shape[1] // TILE):
            part = slice(t * TILE, (t + 1) * TILE)
            block = jnp.dot(vg[...], x[:, part], preferred_element_type=jnp.float32)
            block = block.reshape(n // 2, 2, cols // n, TILE)
            even[:, :, part] = block[:, 0]
            odd[:, :, part] = block[:, 1]

    @pl.when(place[0] == 0)
    def _():
        emit(keep, send)

    @pl.when(place[0] == 1)
    def _():
        emit(send, keep)


def add_kernel(a, b, out):
    out[...] = (a[...] + b[...]).astype(out.dtype)


def fold_kernel(owners, pieces, out, total):
    acc = pieces[0].astype(jnp.float32)
    for i in range(1, pieces.shape[0]):
        acc = acc + pieces[i].astype(jnp.float32)
    total[...] = acc
    span = total.shape[1] // owners
    out[...] = jnp.zeros(out.shape, out.dtype)
    for r in range(owners):
        block = total[:, r * span : (r + 1) * span]
        out[r, :, :span] = block[:8]
        out[r, :, 64 : 64 + span] = block[8:]


def adam_kernel(scale, pieces, m, v, new_m, new_v, update):
    acc = pieces[0]
    for i in range(1, pieces.shape[0]):
        acc = acc + pieces[i]
    span = m.shape[1]
    gradient = jnp.concatenate([acc[:, :span], acc[:, 64 : 64 + span]], axis=0) * scale
    first = 0.9 * m[...] + 0.1 * gradient
    second = 0.95 * v[...] + 0.05 * gradient * gradient
    new_m[...] = first
    new_v[...] = second
    update[...] = first / (1.0 - 0.9**STEP) / (jnp.sqrt(second / (1.0 - 0.95**STEP)) + 1e-08)


def body(layer_input, queries, keys, d_out, doc_start, moment_m, moment_v):
    local_rows = queries.shape[1]
    cycle_size = lax.axis_size("blk")
    cycle_index = lax.axis_index("blk")
    owners = lax.axis_size("grp") * lax.axis_size("dp")
    seq = cycle_size * local_rows
    width, cols = layer_input.shape[2], KV_HEADS * HD
    bf16, f32 = jnp.bfloat16, jnp.float32

    k0 = lax.all_gather(keys[0, :, :HD], "blk", axis=0, tiled=True)
    k1 = lax.all_gather(keys[0, :, HD:], "blk", axis=0, tiled=True)
    high = cycle_index * local_rows // CHUNK
    low = jnp.where(lax.axis_index("grp") == 0, 0, high)
    place = jnp.stack([low, high, cycle_index * local_rows]).astype(jnp.int32)
    partial, own = pl.pallas_call(
        attention_kernel,
        out_shape=(
            jax.ShapeDtypeStruct((seq, cols), bf16),
            jax.ShapeDtypeStruct((local_rows, cols), f32),
        ),
        in_specs=[SCALARS] + [WHOLE] * 5,
        out_specs=(WHOLE, WHOLE),
        scratch_shapes=[
            pltpu.VMEM((KV_HEADS, GROUP * local_rows, HD), bf16),
            pltpu.VMEM((KV_HEADS, GROUP * local_rows, HD), bf16),
            pltpu.VMEM((seq, GROUP * local_rows), f32),
        ],
        compiler_params=PARAMS,
    )(place, doc_start, queries[0], d_out[0], k0, k1)
    pieces = lax.all_to_all(
        partial.reshape(cycle_size, local_rows, cols), "blk", 0, 0, tiled=True
    )

    chips, share = cycle_size // 2, cols // cycle_size
    seat = jnp.stack([lax.rem(cycle_index, 2), cycle_index]).astype(jnp.int32)
    half = jax.ShapeDtypeStruct((chips, share, width), f32)
    keep, send = pl.pallas_call(
        project_kernel,
        out_shape=(half, half),
        in_specs=[SCALARS, WHOLE, WHOLE, WHOLE],
        out_specs=(WHOLE, WHOLE),
        scratch_shapes=[pltpu.VMEM((cols, local_rows), bf16)],
        compiler_params=PARAMS,
    )(seat, own, pieces, layer_input[0])
    other = lax.ppermute(send, "blk", [(i, i ^ 1) for i in range(cycle_size)])
    both = pl.pallas_call(
        add_kernel,
        out_shape=jax.ShapeDtypeStruct((chips, share, width), bf16),
        in_specs=[WHOLE, WHOLE],
        out_specs=WHOLE,
        compiler_params=PARAMS,
    )(keep, other)
    lines = [[c + 2 * i for i in range(chips)] for c in range(2)]
    terms = lax.all_to_all(both, "blk", 0, 0, tiled=True, axis_index_groups=lines)
    sent = pl.pallas_call(
        functools.partial(fold_kernel, owners),
        out_shape=jax.ShapeDtypeStruct((owners, 8, 128), f32),
        in_specs=[WHOLE],
        out_specs=WHOLE,
        scratch_shapes=[pltpu.VMEM((share, width), f32)],
        compiler_params=PARAMS,
    )(terms)
    landed = lax.all_to_all(sent, ("grp", "dp"), 0, 0, tiled=True)
    result = jax.ShapeDtypeStruct(moment_m.shape[::-1], f32)
    outs = pl.pallas_call(
        functools.partial(adam_kernel, 1.0 / math.sqrt(owners * seq)),
        out_shape=(result,) * 3,
        in_specs=[WHOLE] * 3,
        out_specs=(WHOLE,) * 3,
        compiler_params=PARAMS,
    )(landed, moment_m.T, moment_v.T)
    return tuple(o.T for o in outs)


def solution(mesh):
    in_specs = (
        P(("grp", "dp"), "blk", None),
        P(("grp", "dp"), "blk", None),
        P(("grp", "dp"), "blk", None),
        P(("grp", "dp"), "blk", None),
        P(("grp", "dp"), "blk"),
        P(("grp", "dp"), "blk"),
        P(("grp", "dp"), "blk"),
    )
    out_specs = (P(("grp", "dp"), "blk"), P(("grp", "dp"), "blk"), P(("grp", "dp"), "blk"))
    return jax.shard_map(body, mesh=mesh, in_specs=in_specs, out_specs=out_specs, check_vma=False)
```

```python
import functools
import math

import jax
import jax.numpy as jnp
from jax import lax
from jax.experimental import pallas as pl
from jax.experimental.pallas import tpu as pltpu
from jax.sharding import Mesh
from jax.sharding import PartitionSpec as P

KV_HEADS = 2
HD = 128
STEP = 10
GROUP = 7
CHUNK = 512
TILE = 256
masked_score = -1e30
GAIN = HD ** (-0.5) * math.log2(math.e)
WHOLE = pl.BlockSpec(memory_space=pltpu.VMEM)
SCALARS = pl.BlockSpec(memory_space=pltpu.SMEM)
PARAMS = pltpu.CompilerParams(vmem_limit_bytes=24 * 1024 * 1024)


def product(a, b, axis):
    return lax.dot_general(
        a, b, (((1,), (axis,)), ((), ())), preferred_element_type=jnp.float32
    )


def lanes_of_queries(row):
    return jnp.concatenate([row] * GROUP, axis=1)


def local_kernel(place, begin, q, d, k, out, qs, ds):
    rows = q.shape[0]
    width = GROUP * rows

    @pl.when(place[0] == 0)
    def _():
        out[...] = jnp.zeros(out.shape, out.dtype)

    @pl.when(place[0] == 1)
    def _():
        first = lanes_of_queries(begin[...] - place[1])
        query_pos = lanes_of_queries(lax.broadcasted_iota(jnp.int32, (1, rows), 1))
        key_pos = lax.broadcasted_iota(jnp.int32, (rows, width), 0)
        visible = (key_pos >= first) & (key_pos <= query_pos)
        for g in range(KV_HEADS):
            for r in range(GROUP):
                h = g * GROUP + r
                qs[r * rows : (r + 1) * rows, :] = q[:, h * HD : (h + 1) * HD]
                ds[r * rows : (r + 1) * rows, :] = d[:, h * HD : (h + 1) * HD]
            cols = slice(g * HD, (g + 1) * HD)
            x = jnp.where(visible, product(k[:, cols], qs[...], 1) * GAIN, masked_score)
            top = jnp.max(x, axis=0, keepdims=True)
            shift = top + jnp.log2(jnp.sum(jnp.exp2(x - top), axis=0, keepdims=True))
            p = jnp.exp2(x - shift).astype(ds.dtype)
            out[:, cols] = product(p, ds[...], 0).astype(out.dtype)


def long_kernel(place, q, d, other, k, out, own, qs, ds, s):
    seq, rows = k.shape[0], q.shape[0]
    width = GROUP * rows
    first_row, high = place[1], place[2]

    @pl.when(place[0] == 0)
    def _():
        for r in range(GROUP):
            qs[r * rows : (r + 1) * rows, :] = q[:, r * HD : (r + 1) * HD]
            ds[r * rows : (r + 1) * rows, :] = d[:, r * HD : (r + 1) * HD]

    @pl.when(place[0] == 1)
    def _():
        for r in range(GROUP):
            h = GROUP + r
            qs[r * rows : (r + 1) * rows, :] = other[:, r * HD : (r + 1) * HD]
            ds[r * rows : (r + 1) * rows, :] = other[:, h * HD : (h + 1) * HD]

    def chunk_rows(c):
        return pl.ds(pl.multiple_of(c * CHUNK, CHUNK), CHUNK)

    def clear(c, carry):
        out[chunk_rows(c), :] = jnp.zeros((CHUNK, HD), out.dtype)
        return carry

    lax.fori_loop(high + 1, seq // CHUNK, clear, 0)

    def larger(x, top):
        return jnp.maximum(top, jnp.max(x.reshape(CHUNK // 8, 8, width), axis=0))

    def inner(c, top):
        x = product(k[chunk_rows(c), :], qs[...], 1) * GAIN
        s[chunk_rows(c), :] = x
        return larger(x, top)

    top = lax.fori_loop(0, high, inner, jnp.full((8, width), masked_score, jnp.float32))
    query_pos = first_row + lanes_of_queries(lax.broadcasted_iota(jnp.int32, (1, rows), 1))
    key_pos = high * CHUNK + lax.broadcasted_iota(jnp.int32, (CHUNK, width), 0)
    x = product(k[chunk_rows(high), :], qs[...], 1) * GAIN
    x = jnp.where(key_pos <= query_pos, x, masked_score)
    s[chunk_rows(high), :] = x
    top = jnp.max(larger(x, top), axis=0, keepdims=True)

    def weigh(c, total):
        p = jnp.exp2(s[chunk_rows(c), :] - top)
        return total + jnp.sum(p.reshape(CHUNK // 8, 8, width), axis=0)

    total = lax.fori_loop(0, high + 1, weigh, jnp.zeros((8, width), jnp.float32))
    shift = top + jnp.log2(jnp.sum(total, axis=0, keepdims=True))

    def collect(c):
        p = jnp.exp2(s[chunk_rows(c), :] - shift).astype(ds.dtype)
        block = product(p, ds[...], 0)
        out[chunk_rows(c), :] = block.astype(out.dtype)
        return block

    def inner_collect(c, carry):
        collect(c)
        return carry

    lax.fori_loop(0, high, inner_collect, 0)
    block = collect(high)
    for i in range(CHUNK // rows):

        @pl.when(first_row == high * CHUNK + i * rows)
        def _():
            own[...] = block[i * rows : (i + 1) * rows]


def value_kernel(place, own, pieces, short, out):
    total = own[...]
    for i in range(pieces.shape[0]):
        total = total + jnp.where(place[3] == i, 0.0, pieces[i].astype(jnp.float32))
    out[:, :HD] = total.astype(out.dtype)
    out[:, HD:] = short[...]


def project_kernel(place, values, mine, across, beside, corner, out, turned, vg):
    share = out.shape[1]
    rows = values.shape[1]
    group, core = place[0], place[4]
    for c in range(2):
        for g in range(KV_HEADS):
            heads = slice(g * HD, (g + 1) * HD)
            part = values[2 * g + c, :, :HD].astype(jnp.float32)
            turned[c, heads, :] = jnp.transpose(part)
            part = values[2 + c, :, (1 + g) * HD : (2 + g) * HD].astype(jnp.float32)
            turned[2 + c, heads, :] = jnp.transpose(part)
    for j in range(4):
        g = jnp.where(j % 2 == 0, group, 1 - group)
        c = jnp.where(j // 2 == 0, core, 1 - core)
        for i in range(out.shape[0]):
            chunk = pl.ds(pl.multiple_of((2 * i + core) * share, share), share)
            block = turned[2 * g + c, chunk, :].astype(vg.dtype)
            vg[i * share : (i + 1) * share, j * rows : (j + 1) * rows] = block
    for t in range(mine.shape[1] // TILE):
        part = slice(t * TILE, (t + 1) * TILE)
        x = jnp.concatenate(
            [mine[:, part], across[:, part], beside[:, part], corner[:, part]], axis=0
        )
        block = product(vg[...], x, 0)
        out[:, :, part] = block.astype(out.dtype).reshape(out.shape[0], share, TILE)


def fold_kernel(owners, pieces, out, total):
    acc = pieces[0].astype(jnp.float32)
    for i in range(1, pieces.shape[0]):
        acc = acc + pieces[i].astype(jnp.float32)
    total[...] = acc
    span = total.shape[1] // owners
    out[...] = jnp.zeros(out.shape, out.dtype)
    for r in range(owners):
        block = total[:, r * span : (r + 1) * span]
        out[r, :, :span] = block[:8]
        out[r, :, 64 : 64 + span] = block[8:]


def adam_kernel(scale, pieces, m, v, new_m, new_v, update):
    acc = pieces[0]
    for i in range(1, pieces.shape[0]):
        acc = acc + pieces[i]
    span = m.shape[1]
    gradient = jnp.concatenate([acc[:, :span], acc[:, 64 : 64 + span]], axis=0) * scale
    first = 0.9 * m[...] + 0.1 * gradient
    second = 0.95 * v[...] + 0.05 * gradient * gradient
    new_m[...] = first
    new_v[...] = second
    update[...] = first / (1.0 - 0.9**STEP) / (jnp.sqrt(second / (1.0 - 0.95**STEP)) + 1e-08)


def call(kernel, out, scalars, arrays, scratch=(), flops=0):
    many = isinstance(out, tuple)
    return pl.pallas_call(
        kernel,
        out_shape=out,
        in_specs=[SCALARS] * len(scalars) + [WHOLE] * len(arrays),
        out_specs=(WHOLE,) * len(out) if many else WHOLE,
        scratch_shapes=list(scratch),
        compiler_params=PARAMS,
        cost_estimate=pl.CostEstimate(flops=flops, bytes_accessed=0, transcendentals=0),
    )(*scalars, *arrays)


def body(layer_input, queries, keys, d_out, doc_start, moment_m, moment_v):
    rows = queries.shape[1]
    chips, cores = lax.axis_size("x"), lax.axis_size("core")
    owners = lax.axis_size("dp")
    blocks = chips * cores
    seq = blocks * rows
    width, cols = layer_input.shape[2], KV_HEADS * HD
    half, share = width // 2, cols // blocks
    heads = GROUP * HD
    bf16, f32 = jnp.bfloat16, jnp.float32
    shape = jax.ShapeDtypeStruct

    group, core = lax.axis_index("grp"), lax.axis_index("core")
    index = lax.axis_index("x") * cores + core
    first_row = index * rows
    place = jnp.stack([group, first_row, first_row // CHUNK, index, core]).astype(jnp.int32)
    q, d, k = queries[0], d_out[0], keys[0]

    down = [(0, 1)]
    other_k = lax.ppermute(k[:, HD:], "grp", down)
    other = lax.ppermute(jnp.concatenate([q[:, heads:], d[:, heads:]], axis=1), "grp", down)
    short = call(
        local_kernel,
        shape((rows, cols), bf16),
        [place],
        [doc_start, q, d, k],
        [pltpu.VMEM((heads, HD), bf16), pltpu.VMEM((heads, HD), bf16)],
        flops=3 * 10**9,
    )
    lower, upper = layer_input[0, :, :half], layer_input[0, :, half:]
    mine = jnp.where(group == 0, lower, upper)
    theirs = jnp.where(group == 0, upper, lower)
    theirs, other_k, short = lax.optimization_barrier((theirs, other_k, short))
    swap = [(0, 1), (1, 0)]
    across = lax.ppermute(theirs, "grp", swap)
    chosen = jnp.where(group == 0, k[:, :HD], other_k)
    all_keys = lax.all_gather(chosen, ("x", "core"), axis=0, tiled=True)
    partial, own = call(
        long_kernel,
        (shape((seq, HD), bf16), shape((rows, HD), f32)),
        [place],
        [q, d, other, all_keys],
        [
            pltpu.VMEM((heads, HD), bf16),
            pltpu.VMEM((heads, HD), bf16),
            pltpu.VMEM((seq, GROUP * rows), f32),
        ],
        flops=6 * 10**9,
    )
    mine, across, own = lax.optimization_barrier((mine, across, own))
    beside = lax.ppermute(mine, "core", swap)
    corner = lax.ppermute(across, "core", swap)
    pieces = lax.all_to_all(
        partial.reshape(blocks, rows, HD), ("x", "core"), 0, 0, tiled=True
    )
    values = call(value_kernel, shape((rows, HD + cols), bf16), [place], [own, pieces, short])
    values = lax.all_gather(values, ("grp", "core"), axis=0)
    gradient = call(
        project_kernel,
        shape((chips, share, half), bf16),
        [place],
        [values, mine, across, beside, corner],
        [pltpu.VMEM((4, cols, rows), f32), pltpu.VMEM((cols // 2, 4 * rows), bf16)],
    )
    terms = lax.all_to_all(gradient, "x", 0, 0, tiled=True)
    sent = call(
        functools.partial(fold_kernel, owners),
        shape((owners, 8, 128), f32),
        [],
        [terms],
        [pltpu.VMEM((share, half), f32)],
    )
    landed = lax.all_to_all(sent, "dp", 0, 0, tiled=True)
    result = shape(moment_m.shape[::-1], f32)
    total_tokens = 2 * owners * seq
    outs = call(
        functools.partial(adam_kernel, 1.0 / math.sqrt(total_tokens)),
        (result,) * 3,
        [],
        [landed, moment_m.T, moment_v.T],
    )
    return tuple(o.T for o in outs)


def solution(mesh):
    split = mesh.devices.reshape(*mesh.devices.shape[:2], -1, 2)
    mesh = Mesh(split, ("grp", "dp", "x", "core"))
    slots, tokens = ("grp", "dp"), ("x", "core")
    wide, flat = P(slots, tokens, None), P(slots, tokens)
    in_specs = (wide, wide, wide, wide, flat, flat, flat)
    return jax.shard_map(
        body, mesh=mesh, in_specs=in_specs, out_specs=(flat,) * 3, check_vma=False
    )
```

```python
import functools
import math

import jax
import jax.numpy as jnp
from jax import lax
from jax.experimental import pallas as pl
from jax.experimental.pallas import tpu as pltpu
from jax.sharding import Mesh
from jax.sharding import PartitionSpec as P

KV_HEADS = 2
HD = 128
STEP = 10
GROUP = 7
CHUNK = 512
masked_score = -1e30
GAIN = HD ** (-0.5) * math.log2(math.e)
WHOLE = pl.BlockSpec(memory_space=pltpu.VMEM)
SCALARS = pl.BlockSpec(memory_space=pltpu.SMEM)
PARAMS = pltpu.CompilerParams(vmem_limit_bytes=24 * 1024 * 1024)


def product(a, b, axis):
    return lax.dot_general(
        a, b, (((1,), (axis,)), ((), ())), preferred_element_type=jnp.float32
    )


def lanes_of_queries(row):
    return jnp.concatenate([row] * GROUP, axis=1)


def regroup_rows(owners, x, group, mine, theirs):
    rows = x.shape[0]
    half = x.shape[1] // 2
    span = half // owners
    for g in range(2):
        at = slice(0, rows) if g == group else slice(rows, 2 * rows)
        for p in range(owners // 2):
            for parity, out in enumerate((mine, theirs)):
                start = g * half + (2 * p + parity) * span
                out[at, p * span : (p + 1) * span] = x[:, start : start + span]


def pack_kernel(owners, place, begin, q, d, k, x, out, packed, keep, send, qs, ds):
    rows = q.shape[0]
    width = GROUP * rows
    heads = GROUP * HD
    packed[:, :heads] = q[:, heads:]
    packed[:, heads:] = d[:, heads:]
    for group in range(2):
        for low in range(2):

            @pl.when((place[0] == group) & (place[5] == low))
            def _():
                refs = (send, keep) if low else (keep, send)
                regroup_rows(owners, x, group, *refs)

    @pl.when(place[0] == 0)
    def _():
        out[...] = jnp.zeros(out.shape, out.dtype)

    @pl.when(place[0] == 1)
    def _():
        first = lanes_of_queries(begin[...] - place[1])
        query_pos = lanes_of_queries(lax.broadcasted_iota(jnp.int32, (1, rows), 1))
        key_pos = lax.broadcasted_iota(jnp.int32, (rows, width), 0)
        visible = (key_pos >= first) & (key_pos <= query_pos)
        for g in range(KV_HEADS):
            for r in range(GROUP):
                h = g * GROUP + r
                qs[r * rows : (r + 1) * rows, :] = q[:, h * HD : (h + 1) * HD]
                ds[r * rows : (r + 1) * rows, :] = d[:, h * HD : (h + 1) * HD]
            cols = slice(g * HD, (g + 1) * HD)
            x = jnp.where(visible, product(k[:, cols], qs[...], 1) * GAIN, masked_score)
            top = jnp.max(x, axis=0, keepdims=True)
            shift = top + jnp.log2(jnp.sum(jnp.exp2(x - top), axis=0, keepdims=True))
            p = jnp.exp2(x - shift).astype(ds.dtype)
            out[:, cols] = product(p, ds[...], 0).astype(out.dtype)


def long_kernel(place, q, d, other, k, out, own, qs, ds, s):
    seq, rows = k.shape[0], q.shape[0]
    width = GROUP * rows
    first_row, high = place[1], place[2]

    @pl.when(place[0] == 0)
    def _():
        for r in range(GROUP):
            qs[r * rows : (r + 1) * rows, :] = q[:, r * HD : (r + 1) * HD]
            ds[r * rows : (r + 1) * rows, :] = d[:, r * HD : (r + 1) * HD]

    @pl.when(place[0] == 1)
    def _():
        for r in range(GROUP):
            h = GROUP + r
            qs[r * rows : (r + 1) * rows, :] = other[:, r * HD : (r + 1) * HD]
            ds[r * rows : (r + 1) * rows, :] = other[:, h * HD : (h + 1) * HD]

    def chunk_rows(c):
        return pl.ds(pl.multiple_of(c * CHUNK, CHUNK), CHUNK)

    def clear(c, carry):
        out[chunk_rows(c), :] = jnp.zeros((CHUNK, HD), out.dtype)
        return carry

    lax.fori_loop(high + 1, seq // CHUNK, clear, 0)

    def larger(x, top):
        return jnp.maximum(top, jnp.max(x.reshape(CHUNK // 8, 8, width), axis=0))

    def inner(c, top):
        x = product(k[chunk_rows(c), :], qs[...], 1) * GAIN
        s[chunk_rows(c), :] = x
        return larger(x, top)

    top = lax.fori_loop(0, high, inner, jnp.full((8, width), masked_score, jnp.float32))
    query_pos = first_row + lanes_of_queries(lax.broadcasted_iota(jnp.int32, (1, rows), 1))
    key_pos = high * CHUNK + lax.broadcasted_iota(jnp.int32, (CHUNK, width), 0)
    x = product(k[chunk_rows(high), :], qs[...], 1) * GAIN
    x = jnp.where(key_pos <= query_pos, x, masked_score)
    s[chunk_rows(high), :] = x
    top = jnp.max(larger(x, top), axis=0, keepdims=True)

    def weigh(c, total):
        p = jnp.exp2(s[chunk_rows(c), :] - top)
        return total + jnp.sum(p.reshape(CHUNK // 8, 8, width), axis=0)

    total = lax.fori_loop(0, high + 1, weigh, jnp.zeros((8, width), jnp.float32))
    shift = top + jnp.log2(jnp.sum(total, axis=0, keepdims=True))

    def collect(c):
        p = jnp.exp2(s[chunk_rows(c), :] - shift).astype(ds.dtype)
        block = product(p, ds[...], 0)
        out[chunk_rows(c), :] = block.astype(out.dtype)
        return block

    def inner_collect(c, carry):
        collect(c)
        return carry

    lax.fori_loop(0, high, inner_collect, 0)
    block = collect(high)
    for i in range(CHUNK // rows):

        @pl.when(first_row == high * CHUNK + i * rows)
        def _():
            own[...] = block[i * rows : (i + 1) * rows]


def regroup_kernel(keep, got, short, pair, onward, up):
    rows = short.shape[0]
    pair[:rows], pair[rows:] = keep[:rows], got[:rows]
    onward[:rows], onward[rows:] = keep[rows:], got[rows:]
    up[...] = short[:, :HD]


def value_kernel(place, own, pieces, short, got, out):
    total = own[...]
    for i in range(pieces.shape[0]):
        total = total + jnp.where(place[3] == i, 0.0, pieces[i].astype(jnp.float32))
    out[:, :HD] = total.astype(out.dtype)
    out[:, HD:] = jnp.where(place[0] == 0, got[...], short[:, HD:])


def project_kernel(place, values, pair, across, beside, corner, out, turned, vg):
    share = out.shape[1]
    rows = values.shape[1]
    group, core, low = place[0], place[4], place[5]
    for n in range(8):
        g, z, c = n // 4, n // 2 % 2, n % 2
        both = jnp.transpose(values[n].astype(jnp.float32))
        turned[2 * z + c, g * HD : (g + 1) * HD, :] = both[:HD]
        turned[4 + 2 * z + c, g * HD : (g + 1) * HD, :] = both[HD:]
    total = None
    for j, x in enumerate((pair, across, beside, corner)):
        g = group if j % 2 == 0 else 1 - group
        c = core if j // 2 == 0 else 1 - core
        for k in range(2):
            z = low if k == 0 else 1 - low
            for i in range(out.shape[0]):
                chunk = pl.ds(pl.multiple_of((2 * i + core) * share, share), share)
                block = turned[4 * g + 2 * z + c, chunk, :].astype(vg.dtype)
                vg[j, i * share : (i + 1) * share, k * rows : (k + 1) * rows] = block
        part = product(vg[j], x[...], 0)
        total = part if total is None else total + part
    out[...] = total.astype(out.dtype).reshape(out.shape)


def fold_kernel(owners, pieces, out, total):
    acc = pieces[0].astype(jnp.float32)
    for i in range(1, pieces.shape[0]):
        acc = acc + pieces[i].astype(jnp.float32)
    total[...] = acc
    span = total.shape[1] // owners
    out[...] = jnp.zeros(out.shape, out.dtype)
    for r in range(owners):
        block = total[:, r * span : (r + 1) * span]
        out[r, :, :span] = block[:8]
        out[r, :, 64 : 64 + span] = block[8:]


def adam_kernel(scale, pieces, m, v, new_m, new_v, update):
    acc = pieces[0]
    for i in range(1, pieces.shape[0]):
        acc = acc + pieces[i]
    span = m.shape[1]
    gradient = jnp.concatenate([acc[:, :span], acc[:, 64 : 64 + span]], axis=0) * scale
    first = 0.9 * m[...] + 0.1 * gradient
    second = 0.95 * v[...] + 0.05 * gradient * gradient
    new_m[...] = first
    new_v[...] = second
    update[...] = first / (1.0 - 0.9**STEP) / (jnp.sqrt(second / (1.0 - 0.95**STEP)) + 1e-08)


def call(kernel, out, scalars, arrays, scratch=(), flops=0):
    many = isinstance(out, tuple)
    return pl.pallas_call(
        kernel,
        out_shape=out,
        in_specs=[SCALARS] * len(scalars) + [WHOLE] * len(arrays),
        out_specs=(WHOLE,) * len(out) if many else WHOLE,
        scratch_shapes=list(scratch),
        compiler_params=PARAMS,
        cost_estimate=pl.CostEstimate(flops=flops, bytes_accessed=0, transcendentals=0),
    )(*scalars, *arrays)


def body(layer_input, queries, keys, d_out, doc_start, moment_m, moment_v):
    rows = queries.shape[1]
    chips, cores = lax.axis_size("x"), lax.axis_size("core")
    owners = lax.axis_size("dp")
    blocks = chips * cores
    seq = blocks * rows
    width, cols = layer_input.shape[2], KV_HEADS * HD
    quarter, share = width // 4, cols // blocks
    heads = GROUP * HD
    bf16, f32 = jnp.bfloat16, jnp.float32
    shape = jax.ShapeDtypeStruct

    group, low, core = lax.axis_index("grp"), lax.axis_index("zl"), lax.axis_index("core")
    index = lax.axis_index("x") * cores + core
    first_row = index * rows
    place = jnp.stack([group, first_row, first_row // CHUNK, index, core, low]).astype(jnp.int32)
    q, d, k = queries[0], d_out[0], keys[0]

    down, up, swap = [(0, 1)], [(1, 0)], [(0, 1), (1, 0)]
    other_k = lax.ppermute(k, "grp", down)
    block = shape((2 * rows, quarter), bf16)
    short, packed, keep, send = call(
        functools.partial(pack_kernel, 2 * owners),
        (shape((rows, cols), bf16), shape((rows, 2 * heads), bf16), block, block),
        [place],
        [doc_start, q, d, k, layer_input[0]],
        [pltpu.VMEM((heads, HD), bf16), pltpu.VMEM((heads, HD), bf16)],
        flops=3 * 10**9,
    )
    other = lax.ppermute(packed, "grp", down)
    got = lax.ppermute(send, "zl", swap)
    chosen = jnp.where(group == 0, k[:, :HD], other_k[:, HD:])
    all_keys = lax.all_gather(chosen, ("x", "core"), axis=0, tiled=True)
    all_keys, got = lax.optimization_barrier((all_keys, got))
    partial, own = call(
        long_kernel,
        (shape((seq, HD), bf16), shape((rows, HD), f32)),
        [place],
        [q, d, other, all_keys],
        [
            pltpu.VMEM((heads, HD), bf16),
            pltpu.VMEM((heads, HD), bf16),
            pltpu.VMEM((seq, GROUP * rows), f32),
        ],
        flops=6 * 10**9,
    )
    got, own = lax.optimization_barrier((got, own))
    pair, onward, upward = call(
        regroup_kernel, (block, block, shape((rows, HD), bf16)), [], [keep, got, short]
    )
    across = lax.ppermute(onward, "grp", swap)
    beside = lax.ppermute(pair, "core", swap)
    from_short = lax.ppermute(upward, "grp", up)
    corner = lax.ppermute(across, "core", swap)
    pieces = lax.all_to_all(
        partial.reshape(blocks, rows, HD), ("x", "core"), 0, 0, tiled=True
    )
    values = call(
        value_kernel, shape((rows, 2 * HD), bf16), [place], [own, pieces, short, from_short]
    )
    values = lax.all_gather(values, ("grp", "zl", "core"), axis=0)
    gradient = call(
        project_kernel,
        shape((chips, share, quarter), bf16),
        [place],
        [values, pair, across, beside, corner],
        [pltpu.VMEM((8, cols, rows), f32), pltpu.VMEM((4, cols // 2, 2 * rows), bf16)],
    )
    terms = lax.all_to_all(gradient, "x", 0, 0, tiled=True)
    sent = call(
        functools.partial(fold_kernel, owners),
        shape((owners, 8, 128), f32),
        [],
        [terms],
        [pltpu.VMEM((share, quarter), f32)],
    )
    landed = lax.all_to_all(sent, "dp", 0, 0, tiled=True)
    result = shape(moment_m.shape[::-1], f32)
    total_tokens = 4 * owners * seq
    outs = call(
        functools.partial(adam_kernel, 1.0 / math.sqrt(total_tokens)),
        (result,) * 3,
        [],
        [landed, moment_m.T, moment_v.T],
    )
    return tuple(o.T for o in outs)


def solution(mesh):
    groups, copies, blocks = mesh.devices.shape
    split = mesh.devices.reshape(groups, copies // 2, 2, blocks // 2, 2)
    mesh = Mesh(split, ("grp", "dp", "zl", "x", "core"))
    slots, tokens = ("grp", "dp", "zl"), ("x", "core")
    wide, flat = P(slots, tokens, None), P(slots, tokens)
    in_specs = (wide, wide, wide, wide, flat, flat, flat)
    return jax.shard_map(
        body, mesh=mesh, in_specs=in_specs, out_specs=(flat,) * 3, check_vma=False
    )
```

```python
import functools
import math

import jax
import jax.numpy as jnp
from jax import lax
from jax.experimental import pallas as pl
from jax.experimental.pallas import tpu as pltpu
from jax.sharding import Mesh
from jax.sharding import PartitionSpec as P

KV_HEADS = 2
HD = 128
STEP = 10
GROUP = 7
CHUNK = 512
TILE = 256
masked_score = -1e30
GAIN = HD ** (-0.5) * math.log2(math.e)
WHOLE = pl.BlockSpec(memory_space=pltpu.VMEM)
SCALARS = pl.BlockSpec(memory_space=pltpu.SMEM)
PARAMS = pltpu.CompilerParams(vmem_limit_bytes=24 * 1024 * 1024)


def product(a, b, axis):
    return lax.dot_general(
        a, b, (((1,), (axis,)), ((), ())), preferred_element_type=jnp.float32
    )


def lanes_of_queries(row):
    return jnp.concatenate([row] * GROUP, axis=1)


def local_kernel(place, begin, q, d, k, out, qs, ds):
    rows = q.shape[0]
    width = GROUP * rows

    @pl.when(place[0] == 0)
    def _():
        out[...] = jnp.zeros(out.shape, out.dtype)

    @pl.when(place[0] == 1)
    def _():
        first = lanes_of_queries(begin[...] - place[1])
        query_pos = lanes_of_queries(lax.broadcasted_iota(jnp.int32, (1, rows), 1))
        key_pos = lax.broadcasted_iota(jnp.int32, (rows, width), 0)
        visible = (key_pos >= first) & (key_pos <= query_pos)
        for g in range(KV_HEADS):
            for r in range(GROUP):
                h = g * GROUP + r
                qs[r * rows : (r + 1) * rows, :] = q[:, h * HD : (h + 1) * HD]
                ds[r * rows : (r + 1) * rows, :] = d[:, h * HD : (h + 1) * HD]
            cols = slice(g * HD, (g + 1) * HD)
            x = jnp.where(visible, product(k[:, cols], qs[...], 1) * GAIN, masked_score)
            top = jnp.max(x, axis=0, keepdims=True)
            shift = top + jnp.log2(jnp.sum(jnp.exp2(x - top), axis=0, keepdims=True))
            p = jnp.exp2(x - shift).astype(ds.dtype)
            out[:, cols] = product(p, ds[...], 0).astype(out.dtype)


def long_kernel(place, q, d, other, k, out, own, qs, ds, s):
    seq, rows = k.shape[0], q.shape[0]
    width = GROUP * rows
    first_row, high = place[1], place[2]

    @pl.when(place[0] == 0)
    def _():
        for r in range(GROUP):
            qs[r * rows : (r + 1) * rows, :] = q[:, r * HD : (r + 1) * HD]
            ds[r * rows : (r + 1) * rows, :] = d[:, r * HD : (r + 1) * HD]

    @pl.when(place[0] == 1)
    def _():
        for r in range(GROUP):
            h = GROUP + r
            qs[r * rows : (r + 1) * rows, :] = other[:, r * HD : (r + 1) * HD]
            ds[r * rows : (r + 1) * rows, :] = other[:, h * HD : (h + 1) * HD]

    def chunk_rows(c):
        return pl.ds(pl.multiple_of(c * CHUNK, CHUNK), CHUNK)

    def clear(c, carry):
        out[chunk_rows(c), :] = jnp.zeros((CHUNK, HD), out.dtype)
        return carry

    lax.fori_loop(high + 1, seq // CHUNK, clear, 0)

    def absorb(x, top, total):
        x = x.reshape(CHUNK // 8, 8, width)
        larger = jnp.maximum(top, jnp.max(x, axis=0))
        total = total * jnp.exp2(top - larger) + jnp.sum(jnp.exp2(x - larger), axis=0)
        return larger, total

    def inner(c, carry):
        x = product(k[chunk_rows(c), :], qs[...], 1) * GAIN
        s[chunk_rows(c), :] = x
        return absorb(x, *carry)

    empty = jnp.full((8, width), masked_score, jnp.float32), jnp.zeros((8, width), jnp.float32)
    top, total = lax.fori_loop(0, high, inner, empty)
    query_pos = first_row + lanes_of_queries(lax.broadcasted_iota(jnp.int32, (1, rows), 1))
    key_pos = high * CHUNK + lax.broadcasted_iota(jnp.int32, (CHUNK, width), 0)
    x = product(k[chunk_rows(high), :], qs[...], 1) * GAIN
    x = jnp.where(key_pos <= query_pos, x, masked_score)
    s[chunk_rows(high), :] = x
    top, total = absorb(x, top, total)
    most = jnp.max(top, axis=0, keepdims=True)
    total = jnp.sum(total * jnp.exp2(top - most), axis=0, keepdims=True)
    shift = most + jnp.log2(total)

    def collect(c):
        p = jnp.exp2(s[chunk_rows(c), :] - shift).astype(ds.dtype)
        block = product(p, ds[...], 0)
        out[chunk_rows(c), :] = block.astype(out.dtype)
        return block

    def inner_collect(c, carry):
        collect(c)
        return carry

    lax.fori_loop(0, high, inner_collect, 0)
    block = collect(high)
    for i in range(CHUNK // rows):

        @pl.when(first_row == high * CHUNK + i * rows)
        def _():
            own[...] = block[i * rows : (i + 1) * rows]


def value_kernel(place, own, pieces, short, out):
    total = own[...]
    for i in range(pieces.shape[0]):
        total = total + jnp.where(place[3] == i, 0.0, pieces[i].astype(jnp.float32))
    out[:, :HD] = total.astype(out.dtype)
    out[:, HD:] = short[...]


def project_kernel(place, values, mine, across, beside, corner, out, turned, vg):
    share = out.shape[1]
    rows = values.shape[1]
    group, core = place[0], place[4]
    for c in range(2):
        for g in range(KV_HEADS):
            heads = slice(g * HD, (g + 1) * HD)
            part = values[2 * g + c, :, :HD].astype(jnp.float32)
            turned[c, heads, :] = jnp.transpose(part)
            part = values[2 + c, :, (1 + g) * HD : (2 + g) * HD].astype(jnp.float32)
            turned[2 + c, heads, :] = jnp.transpose(part)
    for j in range(4):
        g = jnp.where(j % 2 == 0, group, 1 - group)
        c = jnp.where(j // 2 == 0, core, 1 - core)
        for i in range(out.shape[0]):
            chunk = pl.ds(pl.multiple_of((2 * i + core) * share, share), share)
            block = turned[2 * g + c, chunk, :].astype(vg.dtype)
            vg[i * share : (i + 1) * share, j * rows : (j + 1) * rows] = block
    for t in range(mine.shape[1] // TILE):
        part = slice(t * TILE, (t + 1) * TILE)
        x = jnp.concatenate(
            [mine[:, part], across[:, part], beside[:, part], corner[:, part]], axis=0
        )
        block = product(vg[...], x, 0)
        out[:, :, part] = block.astype(out.dtype).reshape(out.shape[0], share, TILE)


def fold_kernel(owners, pieces, out, total):
    acc = pieces[0].astype(jnp.float32)
    for i in range(1, pieces.shape[0]):
        acc = acc + pieces[i].astype(jnp.float32)
    total[...] = acc
    span = total.shape[1] // owners
    out[...] = jnp.zeros(out.shape, out.dtype)
    for r in range(owners):
        block = total[:, r * span : (r + 1) * span]
        out[r, :, :span] = block[:8]
        out[r, :, 64 : 64 + span] = block[8:]


def adam_kernel(scale, pieces, m, v, new_m, new_v, update):
    acc = pieces[0]
    for i in range(1, pieces.shape[0]):
        acc = acc + pieces[i]
    span = m.shape[1]
    gradient = jnp.concatenate([acc[:, :span], acc[:, 64 : 64 + span]], axis=0) * scale
    first = 0.9 * m[...] + 0.1 * gradient
    second = 0.95 * v[...] + 0.05 * gradient * gradient
    new_m[...] = first
    new_v[...] = second
    update[...] = first / (1.0 - 0.9**STEP) / (jnp.sqrt(second / (1.0 - 0.95**STEP)) + 1e-08)


def call(kernel, out, scalars, arrays, scratch=(), flops=0):
    many = isinstance(out, tuple)
    return pl.pallas_call(
        kernel,
        out_shape=out,
        in_specs=[SCALARS] * len(scalars) + [WHOLE] * len(arrays),
        out_specs=(WHOLE,) * len(out) if many else WHOLE,
        scratch_shapes=list(scratch),
        compiler_params=PARAMS,
        cost_estimate=pl.CostEstimate(flops=flops, bytes_accessed=0, transcendentals=0),
    )(*scalars, *arrays)


def body(layer_input, queries, keys, d_out, doc_start, moment_m, moment_v):
    rows = queries.shape[1]
    chips, cores = lax.axis_size("x"), lax.axis_size("core")
    owners = lax.axis_size("dp")
    blocks = chips * cores
    seq = blocks * rows
    width, cols = layer_input.shape[2], KV_HEADS * HD
    half, share = width // 2, cols // blocks
    heads = GROUP * HD
    bf16, f32 = jnp.bfloat16, jnp.float32
    shape = jax.ShapeDtypeStruct

    group, core = lax.axis_index("grp"), lax.axis_index("core")
    index = lax.axis_index("x") * cores + core
    first_row = index * rows
    place = jnp.stack([group, first_row, first_row // CHUNK, index, core]).astype(jnp.int32)
    q, d, k = queries[0], d_out[0], keys[0]

    down, swap = [(0, 1)], [(0, 1), (1, 0)]
    other_k = lax.ppermute(k, "grp", down)
    other = lax.ppermute(jnp.concatenate([q[:, heads:], d[:, heads:]], axis=1), "grp", down)
    lower, upper = layer_input[0, :, :half], layer_input[0, :, half:]
    mine = jnp.where(group == 0, lower, upper)
    theirs = jnp.where(group == 0, upper, lower)
    across = lax.ppermute(theirs, "grp", swap)
    chosen = jnp.where(group == 0, k[:, :HD], other_k[:, HD:])
    all_keys = lax.all_gather(chosen, ("x", "core"), axis=0, tiled=True)
    partial, own = call(
        long_kernel,
        (shape((seq, HD), bf16), shape((rows, HD), f32)),
        [place],
        [q, d, other, all_keys],
        [
            pltpu.VMEM((heads, HD), bf16),
            pltpu.VMEM((heads, HD), bf16),
            pltpu.VMEM((seq, GROUP * rows), f32),
        ],
        flops=6 * 10**9,
    )
    partial, across = lax.optimization_barrier((partial, across))
    mine, begin, own = lax.optimization_barrier((mine, doc_start, own))
    short = call(
        local_kernel,
        shape((rows, cols), bf16),
        [place],
        [begin, q, d, k],
        [pltpu.VMEM((heads, HD), bf16), pltpu.VMEM((heads, HD), bf16)],
        flops=3 * 10**9,
    )
    beside = lax.ppermute(mine, "core", swap)
    corner = lax.ppermute(across, "core", swap)
    pieces = lax.all_to_all(
        partial.reshape(blocks, rows, HD), ("x", "core"), 0, 0, tiled=True
    )
    values = call(value_kernel, shape((rows, HD + cols), bf16), [place], [own, pieces, short])
    values = lax.all_gather(values, ("grp", "core"), axis=0)
    gradient = call(
        project_kernel,
        shape((chips, share, half), bf16),
        [place],
        [values, mine, across, beside, corner],
        [pltpu.VMEM((4, cols, rows), f32), pltpu.VMEM((cols // 2, 4 * rows), bf16)],
    )
    terms = lax.all_to_all(gradient, "x", 0, 0, tiled=True)
    sent = call(
        functools.partial(fold_kernel, owners),
        shape((owners, 8, 128), f32),
        [],
        [terms],
        [pltpu.VMEM((share, half), f32)],
    )
    landed = lax.all_to_all(sent, "dp", 0, 0, tiled=True)
    result = shape(moment_m.shape[::-1], f32)
    total_tokens = 2 * owners * seq
    outs = call(
        functools.partial(adam_kernel, 1.0 / math.sqrt(total_tokens)),
        (result,) * 3,
        [],
        [landed, moment_m.T, moment_v.T],
    )
    return tuple(o.T for o in outs)


def solution(mesh):
    split = mesh.devices.reshape(*mesh.devices.shape[:2], -1, 2)
    mesh = Mesh(split, ("grp", "dp", "x", "core"))
    slots, tokens = ("grp", "dp"), ("x", "core")
    wide, flat = P(slots, tokens, None), P(slots, tokens)
    in_specs = (wide, wide, wide, wide, flat, flat, flat)
    return jax.shard_map(
        body, mesh=mesh, in_specs=in_specs, out_specs=(flat,) * 3, check_vma=False
    )
```

```python
import functools
import math

import jax
import jax.numpy as jnp
from jax import lax
from jax.experimental import pallas as pl
from jax.experimental.pallas import tpu as pltpu
from jax.sharding import Mesh
from jax.sharding import PartitionSpec as P

KV_HEADS = 2
HD = 128
STEP = 10
GROUP = 7
CHUNK = 512
TILE = 256
masked_score = -1e30
GAIN = HD ** (-0.5) * math.log2(math.e)
WHOLE = pl.BlockSpec(memory_space=pltpu.VMEM)
SCALARS = pl.BlockSpec(memory_space=pltpu.SMEM)
PARAMS = pltpu.CompilerParams(vmem_limit_bytes=24 * 1024 * 1024)


def product(a, b, axis):
    return lax.dot_general(
        a, b, (((1,), (axis,)), ((), ())), preferred_element_type=jnp.float32
    )


def lanes_of_queries(row):
    return jnp.concatenate([row] * GROUP, axis=1)


def by_parity(matrix, share):
    width = matrix.shape[1]
    old = lax.broadcasted_iota(jnp.int32, (width, width), 0)
    new = lax.broadcasted_iota(jnp.int32, (width, width), 1)
    half = width // 2
    within = new % half
    source = (2 * (within // share) + new // half) * share + within % share
    chosen = jnp.where(old == source, 1.0, 0.0).astype(matrix.dtype)
    return product(matrix, chosen, 0).astype(matrix.dtype)


def join(a, b, parity):
    half = a.shape[1] // 2
    part = slice(parity * half, (parity + 1) * half)
    return jnp.concatenate([a[:, part], b[:, part]], axis=1)


def local_kernel(share, place, begin, q, d, k, stay, leave, qs, ds):
    rows = q.shape[0]
    width = GROUP * rows

    @pl.when(place[0] == 0)
    def _():
        stay[...] = jnp.zeros(stay.shape, stay.dtype)
        leave[...] = jnp.zeros(leave.shape, leave.dtype)

    @pl.when(place[0] == 1)
    def _():
        first = lanes_of_queries(begin[...] - place[1])
        query_pos = lanes_of_queries(lax.broadcasted_iota(jnp.int32, (1, rows), 1))
        key_pos = lax.broadcasted_iota(jnp.int32, (rows, width), 0)
        visible = (key_pos >= first) & (key_pos <= query_pos)
        sums = []
        for g in range(KV_HEADS):
            for r in range(GROUP):
                h = g * GROUP + r
                qs[r * rows : (r + 1) * rows, :] = q[:, h * HD : (h + 1) * HD]
                ds[r * rows : (r + 1) * rows, :] = d[:, h * HD : (h + 1) * HD]
            cols = slice(g * HD, (g + 1) * HD)
            x = jnp.where(visible, product(k[:, cols], qs[...], 1) * GAIN, masked_score)
            top = jnp.max(x, axis=0, keepdims=True)
            shift = top + jnp.log2(jnp.sum(jnp.exp2(x - top), axis=0, keepdims=True))
            p = jnp.exp2(x - shift).astype(ds.dtype)
            sums.append(product(p, by_parity(ds[...], share), 0))
        even, odd = (join(*sums, parity).astype(stay.dtype) for parity in range(2))
        stay[...] = jnp.where(place[4] == 0, even, odd)
        leave[...] = jnp.where(place[4] == 0, odd, even)


def long_kernel(share, place, q, d, other, k, out, qs, ds, s):
    seq, rows = k.shape[0], q.shape[0]
    width = GROUP * rows
    first_row, high = place[1], place[2]

    @pl.when(place[0] == 0)
    def _():
        for r in range(GROUP):
            qs[r * rows : (r + 1) * rows, :] = q[:, r * HD : (r + 1) * HD]
            ds[r * rows : (r + 1) * rows, :] = d[:, r * HD : (r + 1) * HD]

    @pl.when(place[0] == 1)
    def _():
        for r in range(GROUP):
            h = GROUP + r
            qs[r * rows : (r + 1) * rows, :] = other[:, r * HD : (r + 1) * HD]
            ds[r * rows : (r + 1) * rows, :] = other[:, h * HD : (h + 1) * HD]

    ds[...] = by_parity(ds[...], share)

    def chunk_rows(c):
        return pl.ds(pl.multiple_of(c * CHUNK, CHUNK), CHUNK)

    def clear(c, carry):
        out[chunk_rows(c), :] = jnp.zeros((CHUNK, HD), out.dtype)
        return carry

    lax.fori_loop(high + 1, seq // CHUNK, clear, 0)

    def absorb(x, top, total):
        x = x.reshape(CHUNK // 8, 8, width)
        larger = jnp.maximum(top, jnp.max(x, axis=0))
        total = total * jnp.exp2(top - larger) + jnp.sum(jnp.exp2(x - larger), axis=0)
        return larger, total

    def inner(c, carry):
        x = product(k[chunk_rows(c), :], qs[...], 1) * GAIN
        s[chunk_rows(c), :] = x
        return absorb(x, *carry)

    empty = jnp.full((8, width), masked_score, jnp.float32), jnp.zeros((8, width), jnp.float32)
    top, total = lax.fori_loop(0, high, inner, empty)
    query_pos = first_row + lanes_of_queries(lax.broadcasted_iota(jnp.int32, (1, rows), 1))
    key_pos = high * CHUNK + lax.broadcasted_iota(jnp.int32, (CHUNK, width), 0)
    x = product(k[chunk_rows(high), :], qs[...], 1) * GAIN
    x = jnp.where(key_pos <= query_pos, x, masked_score)
    s[chunk_rows(high), :] = x
    top, total = absorb(x, top, total)
    most = jnp.max(top, axis=0, keepdims=True)
    total = jnp.sum(total * jnp.exp2(top - most), axis=0, keepdims=True)
    shift = most + jnp.log2(total)

    def collect(c, carry):
        p = jnp.exp2(s[chunk_rows(c), :] - shift).astype(ds.dtype)
        block = product(p, ds[...], 0)
        for i in range(0, CHUNK // rows, 2):
            pair = [block[(i + n) * rows : (i + n + 1) * rows] for n in range(2)]
            for parity in range(2):
                at = pl.ds(pl.multiple_of(c * CHUNK + (i + parity) * rows, rows), rows)
                out[at, :] = join(*pair, parity).astype(out.dtype)
        return carry

    lax.fori_loop(0, high + 1, collect, 0)


def value_kernel(pieces, stay, got, out):
    total = pieces[0].astype(jnp.float32)
    for i in range(1, pieces.shape[0]):
        total = total + pieces[i].astype(jnp.float32)
    out[:, :HD] = total.astype(out.dtype)
    out[:, HD : 2 * HD] = stay[...]
    out[:, 2 * HD :] = got[...]


def project_kernel(place, values, mine, across, beside, corner, out, turned, vg):
    share = out.shape[1]
    rows = values.shape[1]
    group, core = place[0], place[4]
    half = HD // 2
    for g in range(KV_HEADS):
        part = jnp.transpose(values[g, :, :HD].astype(jnp.float32))
        for c in range(2):
            turned[c, g * half : (g + 1) * half, :] = part[c * half : (c + 1) * half]
    for n in range(2):
        part = values[1, :, (1 + n) * HD : (2 + n) * HD].astype(jnp.float32)
        turned[2 + n] = jnp.transpose(part)
    for j in range(4):
        g = group if j % 2 == 0 else 1 - group
        c = core if j // 2 == 0 else 1 - core
        block = turned[jnp.where(g == 0, c, 2 + j // 2)]
        vg[:, j * rows : (j + 1) * rows] = block.astype(vg.dtype)
    for t in range(mine.shape[1] // TILE):
        part = slice(t * TILE, (t + 1) * TILE)
        x = jnp.concatenate(
            [mine[:, part], across[:, part], beside[:, part], corner[:, part]], axis=0
        )
        block = product(vg[...], x, 0)
        out[:, :, part] = block.astype(out.dtype).reshape(out.shape[0], share, TILE)


def fold_kernel(owners, pieces, out, total):
    acc = pieces[0].astype(jnp.float32)
    for i in range(1, pieces.shape[0]):
        acc = acc + pieces[i].astype(jnp.float32)
    total[...] = acc
    span = total.shape[1] // owners
    out[...] = jnp.zeros(out.shape, out.dtype)
    for r in range(owners):
        block = total[:, r * span : (r + 1) * span]
        out[r, :, :span] = block[:8]
        out[r, :, 64 : 64 + span] = block[8:]


def adam_kernel(scale, pieces, m, v, new_m, new_v, update):
    acc = pieces[0]
    for i in range(1, pieces.shape[0]):
        acc = acc + pieces[i]
    span = m.shape[1]
    gradient = jnp.concatenate([acc[:, :span], acc[:, 64 : 64 + span]], axis=0) * scale
    first = 0.9 * m[...] + 0.1 * gradient
    second = 0.95 * v[...] + 0.05 * gradient * gradient
    new_m[...] = first
    new_v[...] = second
    update[...] = first / (1.0 - 0.9**STEP) / (jnp.sqrt(second / (1.0 - 0.95**STEP)) + 1e-08)


def call(kernel, out, scalars, arrays, scratch=(), flops=0):
    many = isinstance(out, tuple)
    return pl.pallas_call(
        kernel,
        out_shape=out,
        in_specs=[SCALARS] * len(scalars) + [WHOLE] * len(arrays),
        out_specs=(WHOLE,) * len(out) if many else WHOLE,
        scratch_shapes=list(scratch),
        compiler_params=PARAMS,
        cost_estimate=pl.CostEstimate(flops=flops, bytes_accessed=0, transcendentals=0),
    )(*scalars, *arrays)


def body(layer_input, queries, keys, d_out, doc_start, moment_m, moment_v):
    rows = queries.shape[1]
    chips, cores = lax.axis_size("x"), lax.axis_size("core")
    owners = lax.axis_size("dp")
    blocks = chips * cores
    seq = blocks * rows
    width, cols = layer_input.shape[2], KV_HEADS * HD
    half, share = width // 2, cols // blocks
    heads = GROUP * HD
    bf16, f32 = jnp.bfloat16, jnp.float32
    shape = jax.ShapeDtypeStruct

    group, core = lax.axis_index("grp"), lax.axis_index("core")
    index = lax.axis_index("x") * cores + core
    first_row = index * rows
    place = jnp.stack([group, first_row, first_row // CHUNK, index, core]).astype(jnp.int32)
    q, d, k = queries[0], d_out[0], keys[0]

    down, swap = [(0, 1)], [(0, 1), (1, 0)]
    other_k = lax.ppermute(k, "grp", down)
    other = lax.ppermute(jnp.concatenate([q[:, heads:], d[:, heads:]], axis=1), "grp", down)
    lower, upper = layer_input[0, :, :half], layer_input[0, :, half:]
    mine = jnp.where(group == 0, lower, upper)
    theirs = jnp.where(group == 0, upper, lower)
    across = lax.ppermute(theirs, "grp", swap)
    chosen = jnp.where(group == 0, k[:, :HD], other_k[:, HD:])
    all_keys = lax.all_gather(chosen, ("x", "core"), axis=0, tiled=True)
    partial = call(
        functools.partial(long_kernel, share),
        shape((seq, HD), bf16),
        [place],
        [q, d, other, all_keys],
        [
            pltpu.VMEM((heads, HD), bf16),
            pltpu.VMEM((heads, HD), bf16),
            pltpu.VMEM((seq, GROUP * rows), f32),
        ],
        flops=6 * 10**9,
    )
    partial, across, mine, begin = lax.optimization_barrier((partial, across, mine, doc_start))
    square = shape((rows, HD), bf16)
    stay, leave = call(
        functools.partial(local_kernel, share),
        (square, square),
        [place],
        [begin, q, d, k],
        [pltpu.VMEM((heads, HD), bf16), pltpu.VMEM((heads, HD), bf16)],
        flops=3 * 10**9,
    )
    beside = lax.ppermute(mine, "core", swap)
    corner = lax.ppermute(across, "core", swap)
    got = lax.ppermute(leave, "core", swap)
    pieces = lax.all_to_all(
        partial.reshape(blocks, rows, HD), ("x", "core"), 0, 0, tiled=True
    )
    values = call(value_kernel, shape((rows, 3 * HD), bf16), [], [pieces, stay, got])
    values = lax.all_gather(values, "grp", axis=0)
    gradient = call(
        project_kernel,
        shape((chips, share, half), bf16),
        [place],
        [values, mine, across, beside, corner],
        [pltpu.VMEM((4, cols // 2, rows), f32), pltpu.VMEM((cols // 2, 4 * rows), bf16)],
    )
    terms = lax.all_to_all(gradient, "x", 0, 0, tiled=True)
    sent = call(
        functools.partial(fold_kernel, owners),
        shape((owners, 8, 128), f32),
        [],
        [terms],
        [pltpu.VMEM((share, half), f32)],
    )
    landed = lax.all_to_all(sent, "dp", 0, 0, tiled=True)
    result = shape(moment_m.shape[::-1], f32)
    total_tokens = 2 * owners * seq
    outs = call(
        functools.partial(adam_kernel, 1.0 / math.sqrt(total_tokens)),
        (result,) * 3,
        [],
        [landed, moment_m.T, moment_v.T],
    )
    return tuple(o.T for o in outs)


def solution(mesh):
    split = mesh.devices.reshape(*mesh.devices.shape[:2], -1, 2)
    mesh = Mesh(split, ("grp", "dp", "x", "core"))
    slots, tokens = ("grp", "dp"), ("x", "core")
    wide, flat = P(slots, tokens, None), P(slots, tokens)
    in_specs = (wide, wide, wide, wide, flat, flat, flat)
    return jax.shard_map(
        body, mesh=mesh, in_specs=in_specs, out_specs=(flat,) * 3, check_vma=False
    )
```

```python
import functools
import math

import jax
import jax.numpy as jnp
from jax import lax
from jax.experimental import pallas as pl
from jax.experimental.pallas import tpu as pltpu
from jax.sharding import Mesh
from jax.sharding import PartitionSpec as P

KV_HEADS = 2
HD = 128
STEP = 10
GROUP = 7
CHUNK = 512
masked_score = -1e30
GAIN = HD ** (-0.5) * math.log2(math.e)
WHOLE = pl.BlockSpec(memory_space=pltpu.VMEM)
SCALARS = pl.BlockSpec(memory_space=pltpu.SMEM)
PARAMS = pltpu.CompilerParams(vmem_limit_bytes=24 * 1024 * 1024)


def product(a, b, axis):
    return lax.dot_general(
        a, b, (((1,), (axis,)), ((), ())), preferred_element_type=jnp.float32
    )


def lanes_of_queries(row):
    return jnp.concatenate([row] * GROUP, axis=1)


def by_parity(matrix, share):
    width = matrix.shape[1]
    old = lax.broadcasted_iota(jnp.int32, (width, width), 0)
    new = lax.broadcasted_iota(jnp.int32, (width, width), 1)
    half = width // 2
    within = new % half
    source = (2 * (within // share) + new // half) * share + within % share
    chosen = jnp.where(old == source, 1.0, 0.0).astype(matrix.dtype)
    return product(matrix, chosen, 0).astype(matrix.dtype)


def join(a, b, parity):
    half = a.shape[1] // 2
    part = slice(parity * half, (parity + 1) * half)
    return jnp.concatenate([a[:, part], b[:, part]], axis=1)


def local_kernel(share, place, begin, q, d, k, stay, leave, qs, ds):
    rows = q.shape[0]
    width = GROUP * rows

    @pl.when(place[0] == 0)
    def _():
        stay[...] = jnp.zeros(stay.shape, stay.dtype)
        leave[...] = jnp.zeros(leave.shape, leave.dtype)

    @pl.when(place[0] == 1)
    def _():
        first = lanes_of_queries(begin[...] - place[1])
        query_pos = lanes_of_queries(lax.broadcasted_iota(jnp.int32, (1, rows), 1))
        key_pos = lax.broadcasted_iota(jnp.int32, (rows, width), 0)
        visible = (key_pos >= first) & (key_pos <= query_pos)
        sums = []
        for g in range(KV_HEADS):
            for r in range(GROUP):
                h = g * GROUP + r
                qs[r * rows : (r + 1) * rows, :] = q[:, h * HD : (h + 1) * HD]
                ds[r * rows : (r + 1) * rows, :] = d[:, h * HD : (h + 1) * HD]
            cols = slice(g * HD, (g + 1) * HD)
            x = jnp.where(visible, product(k[:, cols], qs[...], 1) * GAIN, masked_score)
            top = jnp.max(x, axis=0, keepdims=True)
            shift = top + jnp.log2(jnp.sum(jnp.exp2(x - top), axis=0, keepdims=True))
            p = jnp.exp2(x - shift).astype(ds.dtype)
            sums.append(product(p, by_parity(ds[...], share), 0))
        even, odd = (join(*sums, parity).astype(stay.dtype) for parity in range(2))
        stay[...] = jnp.where(place[4] == 0, even, odd)
        leave[...] = jnp.where(place[4] == 0, odd, even)


def long_kernel(share, place, q, d, other, k, out, qs, ds, s):
    seq, rows = k.shape[0], q.shape[0]
    width = GROUP * rows
    first_row, high = place[1], place[2]

    @pl.when(place[0] == 0)
    def _():
        for r in range(GROUP):
            qs[r * rows : (r + 1) * rows, :] = q[:, r * HD : (r + 1) * HD]
            ds[r * rows : (r + 1) * rows, :] = d[:, r * HD : (r + 1) * HD]

    @pl.when(place[0] == 1)
    def _():
        for r in range(GROUP):
            h = GROUP + r
            qs[r * rows : (r + 1) * rows, :] = other[:, r * HD : (r + 1) * HD]
            ds[r * rows : (r + 1) * rows, :] = other[:, h * HD : (h + 1) * HD]

    ds[...] = by_parity(ds[...], share)

    def chunk_rows(c):
        return pl.ds(pl.multiple_of(c * CHUNK, CHUNK), CHUNK)

    def clear(c, carry):
        out[chunk_rows(c), :] = jnp.zeros((CHUNK, HD), out.dtype)
        return carry

    lax.fori_loop(high + 1, seq // CHUNK, clear, 0)

    def absorb(x, top, total):
        x = x.reshape(CHUNK // 8, 8, width)
        larger = jnp.maximum(top, jnp.max(x, axis=0))
        total = total * jnp.exp2(top - larger) + jnp.sum(jnp.exp2(x - larger), axis=0)
        return larger, total

    def inner(c, carry):
        x = product(k[chunk_rows(c), :], qs[...], 1) * GAIN
        s[chunk_rows(c), :] = x
        return absorb(x, *carry)

    empty = jnp.full((8, width), masked_score, jnp.float32), jnp.zeros((8, width), jnp.float32)
    top, total = lax.fori_loop(0, high, inner, empty)
    query_pos = first_row + lanes_of_queries(lax.broadcasted_iota(jnp.int32, (1, rows), 1))
    key_pos = high * CHUNK + lax.broadcasted_iota(jnp.int32, (CHUNK, width), 0)
    x = product(k[chunk_rows(high), :], qs[...], 1) * GAIN
    x = jnp.where(key_pos <= query_pos, x, masked_score)
    s[chunk_rows(high), :] = x
    top, total = absorb(x, top, total)
    most = jnp.max(top, axis=0, keepdims=True)
    total = jnp.sum(total * jnp.exp2(top - most), axis=0, keepdims=True)
    shift = most + jnp.log2(total)

    def collect(c, carry):
        p = jnp.exp2(s[chunk_rows(c), :] - shift).astype(ds.dtype)
        block = product(p, ds[...], 0)
        for i in range(0, CHUNK // rows, 2):
            pair = [block[(i + n) * rows : (i + n + 1) * rows] for n in range(2)]
            for parity in range(2):
                at = pl.ds(pl.multiple_of(c * CHUNK + (i + parity) * rows, rows), rows)
                out[at, :] = join(*pair, parity).astype(out.dtype)
        return carry

    lax.fori_loop(0, high + 1, collect, 0)


def value_kernel(pieces, stay, got, out):
    total = pieces[0].astype(jnp.float32)
    for i in range(1, pieces.shape[0]):
        total = total + pieces[i].astype(jnp.float32)
    out[:, :HD] = total.astype(out.dtype)
    out[:, HD : 2 * HD] = stay[...]
    out[:, 2 * HD :] = got[...]


def project_kernel(place, values, mine, across, beside, corner, out, turned, vg):
    share = out.shape[2]
    rows = values.shape[1]
    group, core = place[0], place[4]
    half = HD // 2
    for g in range(KV_HEADS):
        part = jnp.transpose(values[g, :, :HD].astype(jnp.float32))
        for c in range(2):
            turned[c, g * half : (g + 1) * half, :] = part[c * half : (c + 1) * half]
    for n in range(2):
        part = values[1, :, (1 + n) * HD : (2 + n) * HD].astype(jnp.float32)
        turned[2 + n] = jnp.transpose(part)
    for j in range(4):
        g = group if j % 2 == 0 else 1 - group
        c = core if j // 2 == 0 else 1 - core
        block = turned[jnp.where(g == 0, c, 2 + j // 2)]
        vg[:, j * rows : (j + 1) * rows] = block.astype(vg.dtype)
    chips, stripes, _, span = out.shape
    for t in range(0, stripes, 2):
        part = slice(t * span, (t + 2) * span)
        x = jnp.concatenate(
            [mine[:, part], across[:, part], beside[:, part], corner[:, part]], axis=0
        )
        block = product(vg[...], x, 0)
        for n in range(2):
            piece = block[:, n * span : (n + 1) * span].astype(out.dtype)
            out[:, t + n] = piece.reshape(chips, share, span)


def fold_kernel(owners, pieces, out, total):
    acc = pieces[0].astype(jnp.float32)
    for i in range(1, pieces.shape[0]):
        acc = acc + pieces[i].astype(jnp.float32)
    total[...] = acc
    span = total.shape[1] // owners
    out[...] = jnp.zeros(out.shape, out.dtype)
    for r in range(owners):
        block = total[:, r * span : (r + 1) * span]
        out[r, :, :span] = block[:8]
        out[r, :, 64 : 64 + span] = block[8:]


def adam_kernel(scale, pieces, m, v, new_m, new_v, update):
    acc = pieces[0]
    for i in range(1, pieces.shape[0]):
        acc = acc + pieces[i]
    span = m.shape[1]
    gradient = jnp.concatenate([acc[:, :span], acc[:, 64 : 64 + span]], axis=0) * scale
    first = 0.9 * m[...] + 0.1 * gradient
    second = 0.95 * v[...] + 0.05 * gradient * gradient
    new_m[...] = first
    new_v[...] = second
    update[...] = first / (1.0 - 0.9**STEP) / (jnp.sqrt(second / (1.0 - 0.95**STEP)) + 1e-08)


def call(kernel, out, scalars, arrays, scratch=(), flops=0):
    many = isinstance(out, tuple)
    return pl.pallas_call(
        kernel,
        out_shape=out,
        in_specs=[SCALARS] * len(scalars) + [WHOLE] * len(arrays),
        out_specs=(WHOLE,) * len(out) if many else WHOLE,
        scratch_shapes=list(scratch),
        compiler_params=PARAMS,
        cost_estimate=pl.CostEstimate(flops=flops, bytes_accessed=0, transcendentals=0),
    )(*scalars, *arrays)


def body(layer_input, queries, keys, d_out, doc_start, moment_m, moment_v):
    rows = queries.shape[1]
    chips, cores = lax.axis_size("x"), lax.axis_size("core")
    stripes, owners = lax.axis_size("yh"), lax.axis_size("z")
    blocks = chips * cores
    seq = blocks * rows
    width, cols = layer_input.shape[2], KV_HEADS * HD
    half, share = width // 2, cols // blocks
    heads = GROUP * HD
    bf16, f32 = jnp.bfloat16, jnp.float32
    shape = jax.ShapeDtypeStruct

    group, core = lax.axis_index("grp"), lax.axis_index("core")
    index = lax.axis_index("x") * cores + core
    first_row = index * rows
    place = jnp.stack([group, first_row, first_row // CHUNK, index, core]).astype(jnp.int32)
    q, d, k = queries[0], d_out[0], keys[0]

    down, swap = [(0, 1)], [(0, 1), (1, 0)]
    other_k = lax.ppermute(k, "grp", down)
    other = lax.ppermute(jnp.concatenate([q[:, heads:], d[:, heads:]], axis=1), "grp", down)
    lower, upper = layer_input[0, :, :half], layer_input[0, :, half:]
    mine = jnp.where(group == 0, lower, upper)
    theirs = jnp.where(group == 0, upper, lower)
    across = lax.ppermute(theirs, "grp", swap)
    chosen = jnp.where(group == 0, k[:, :HD], other_k[:, HD:])
    all_keys = lax.all_gather(chosen, ("x", "core"), axis=0, tiled=True)
    partial = call(
        functools.partial(long_kernel, share),
        shape((seq, HD), bf16),
        [place],
        [q, d, other, all_keys],
        [
            pltpu.VMEM((heads, HD), bf16),
            pltpu.VMEM((heads, HD), bf16),
            pltpu.VMEM((seq, GROUP * rows), f32),
        ],
        flops=6 * 10**9,
    )
    partial, across, mine, begin = lax.optimization_barrier((partial, across, mine, doc_start))
    square = shape((rows, HD), bf16)
    stay, leave = call(
        functools.partial(local_kernel, share),
        (square, square),
        [place],
        [begin, q, d, k],
        [pltpu.VMEM((heads, HD), bf16), pltpu.VMEM((heads, HD), bf16)],
        flops=3 * 10**9,
    )
    beside = lax.ppermute(mine, "core", swap)
    corner = lax.ppermute(across, "core", swap)
    got = lax.ppermute(leave, "core", swap)
    pieces = lax.all_to_all(
        partial.reshape(blocks, rows, HD), ("x", "core"), 0, 0, tiled=True
    )
    values = call(value_kernel, shape((rows, 3 * HD), bf16), [], [pieces, stay, got])
    values = lax.all_gather(values, "grp", axis=0)
    gradient = call(
        project_kernel,
        shape((chips, stripes, share, half // stripes), bf16),
        [place],
        [values, mine, across, beside, corner],
        [pltpu.VMEM((4, cols // 2, rows), f32), pltpu.VMEM((cols // 2, 4 * rows), bf16)],
    )
    gradient = gradient.reshape(chips * stripes, share, half // stripes)
    terms = lax.all_to_all(gradient, ("x", "yh"), 0, 0, tiled=True)
    sent = call(
        functools.partial(fold_kernel, owners),
        shape((owners, 8, 128), f32),
        [],
        [terms],
        [pltpu.VMEM((share, half // stripes), f32)],
    )
    landed = lax.all_to_all(sent, "z", 0, 0, tiled=True)
    result = shape(moment_m.shape[::-1], f32)
    total_tokens = 2 * stripes * owners * seq
    outs = call(
        functools.partial(adam_kernel, 1.0 / math.sqrt(total_tokens)),
        (result,) * 3,
        [],
        [landed, moment_m.T, moment_v.T],
    )
    return tuple(o.T for o in outs)


def solution(mesh):
    groups, copies, blocks = mesh.devices.shape
    split = mesh.devices.reshape(groups, 4, copies // 4, blocks // 2, 2)
    mesh = Mesh(split, ("grp", "yh", "z", "x", "core"))
    slots, tokens = ("grp", "yh", "z"), ("x", "core")
    wide, flat = P(slots, tokens, None), P(slots, tokens)
    in_specs = (wide, wide, wide, wide, flat, flat, flat)
    return jax.shard_map(
        body, mesh=mesh, in_specs=in_specs, out_specs=(flat,) * 3, check_vma=False
    )
```

```python
import functools
import math

import jax
import jax.numpy as jnp
from jax import lax
from jax.experimental import pallas as pl
from jax.experimental.pallas import tpu as pltpu
from jax.sharding import Mesh
from jax.sharding import PartitionSpec as P

KV_HEADS = 2
HD = 128
STEP = 10
GROUP = 7
CHUNK = 512
masked_score = -1e30
GAIN = HD ** (-0.5) * math.log2(math.e)
WHOLE = pl.BlockSpec(memory_space=pltpu.VMEM)
SCALARS = pl.BlockSpec(memory_space=pltpu.SMEM)
PARAMS = pltpu.CompilerParams(vmem_limit_bytes=24 * 1024 * 1024)


def product(a, b, axis):
    return lax.dot_general(
        a, b, (((1,), (axis,)), ((), ())), preferred_element_type=jnp.float32
    )


def lanes_of_queries(row):
    return jnp.concatenate([row] * GROUP, axis=1)


def by_parity(matrix, share):
    width = matrix.shape[1]
    old = lax.broadcasted_iota(jnp.int32, (width, width), 0)
    new = lax.broadcasted_iota(jnp.int32, (width, width), 1)
    half = width // 2
    within = new % half
    source = (2 * (within // share) + new // half) * share + within % share
    chosen = jnp.where(old == source, 1.0, 0.0).astype(matrix.dtype)
    return product(matrix, chosen, 0).astype(matrix.dtype)


def join(a, b, parity):
    half = a.shape[1] // 2
    part = slice(parity * half, (parity + 1) * half)
    return jnp.concatenate([a[:, part], b[:, part]], axis=1)


def local_kernel(share, place, begin, q, d, k, stay, leave, qs, ds):
    rows = q.shape[0]
    width = GROUP * rows

    @pl.when(place[0] == 0)
    def _():
        stay[...] = jnp.zeros(stay.shape, stay.dtype)
        leave[...] = jnp.zeros(leave.shape, leave.dtype)

    @pl.when(place[0] == 1)
    def _():
        first = lanes_of_queries(begin[...] - place[1])
        query_pos = lanes_of_queries(lax.broadcasted_iota(jnp.int32, (1, rows), 1))
        key_pos = lax.broadcasted_iota(jnp.int32, (rows, width), 0)
        visible = (key_pos >= first) & (key_pos <= query_pos)
        sums = []
        for g in range(KV_HEADS):
            for r in range(GROUP):
                h = g * GROUP + r
                qs[r * rows : (r + 1) * rows, :] = q[:, h * HD : (h + 1) * HD]
                ds[r * rows : (r + 1) * rows, :] = d[:, h * HD : (h + 1) * HD]
            cols = slice(g * HD, (g + 1) * HD)
            x = jnp.where(visible, product(k[:, cols], qs[...], 1) * GAIN, masked_score)
            top = jnp.max(x, axis=0, keepdims=True)
            shift = top + jnp.log2(jnp.sum(jnp.exp2(x - top), axis=0, keepdims=True))
            p = jnp.exp2(x - shift).astype(ds.dtype)
            sums.append(product(p, by_parity(ds[...], share), 0))
        even, odd = (join(*sums, parity).astype(stay.dtype) for parity in range(2))
        stay[...] = jnp.where(place[4] == 0, even, odd)
        leave[...] = jnp.where(place[4] == 0, odd, even)


def long_kernel(share, place, q, d, other, k, out, qs, ds, s):
    seq, rows = k.shape[0], q.shape[0]
    width = GROUP * rows
    first_row, high = place[1], place[2]

    @pl.when(place[0] == 0)
    def _():
        for r in range(GROUP):
            qs[r * rows : (r + 1) * rows, :] = q[:, r * HD : (r + 1) * HD]
            ds[r * rows : (r + 1) * rows, :] = d[:, r * HD : (r + 1) * HD]

    @pl.when(place[0] == 1)
    def _():
        for r in range(GROUP):
            h = GROUP + r
            qs[r * rows : (r + 1) * rows, :] = other[:, r * HD : (r + 1) * HD]
            ds[r * rows : (r + 1) * rows, :] = other[:, h * HD : (h + 1) * HD]

    ds[...] = by_parity(ds[...], share)

    def chunk_rows(c):
        return pl.ds(pl.multiple_of(c * CHUNK, CHUNK), CHUNK)

    def clear(c, carry):
        out[chunk_rows(c), :] = jnp.zeros((CHUNK, HD), out.dtype)
        return carry

    lax.fori_loop(high + 1, seq // CHUNK, clear, 0)

    def absorb(x, top, total):
        x = x.reshape(CHUNK // 8, 8, width)
        larger = jnp.maximum(top, jnp.max(x, axis=0))
        total = total * jnp.exp2(top - larger) + jnp.sum(jnp.exp2(x - larger), axis=0)
        return larger, total

    def inner(c, carry):
        x = product(k[chunk_rows(c), :], qs[...], 1) * GAIN
        s[chunk_rows(c), :] = x
        return absorb(x, *carry)

    empty = jnp.full((8, width), masked_score, jnp.float32), jnp.zeros((8, width), jnp.float32)
    top, total = lax.fori_loop(0, high, inner, empty)
    query_pos = first_row + lanes_of_queries(lax.broadcasted_iota(jnp.int32, (1, rows), 1))
    key_pos = high * CHUNK + lax.broadcasted_iota(jnp.int32, (CHUNK, width), 0)
    x = product(k[chunk_rows(high), :], qs[...], 1) * GAIN
    x = jnp.where(key_pos <= query_pos, x, masked_score)
    s[chunk_rows(high), :] = x
    top, total = absorb(x, top, total)
    most = jnp.max(top, axis=0, keepdims=True)
    total = jnp.sum(total * jnp.exp2(top - most), axis=0, keepdims=True)
    shift = most + jnp.log2(total)

    def collect(c, carry):
        p = jnp.exp2(s[chunk_rows(c), :] - shift).astype(ds.dtype)
        block = product(p, ds[...], 0)
        for i in range(0, CHUNK // rows, 2):
            pair = [block[(i + n) * rows : (i + n + 1) * rows] for n in range(2)]
            for parity in range(2):
                at = pl.ds(pl.multiple_of(c * CHUNK + (i + parity) * rows, rows), rows)
                out[at, :] = join(*pair, parity).astype(out.dtype)
        return carry

    lax.fori_loop(0, high + 1, collect, 0)


def value_kernel(pieces, stay, got, out):
    total = pieces[0].astype(jnp.float32)
    for i in range(1, pieces.shape[0]):
        total = total + pieces[i].astype(jnp.float32)
    out[:, :HD] = total.astype(out.dtype)
    out[:, HD : 2 * HD] = stay[...]
    out[:, 2 * HD :] = got[...]


def project_kernel(place, values, mine, across, beside, corner, out, turned, vg):
    rows = values.shape[1]
    group, core = place[0], place[4]
    half = HD // 2
    for g in range(KV_HEADS):
        part = jnp.transpose(values[g, :, :HD].astype(jnp.float32))
        for c in range(2):
            turned[c, g * half : (g + 1) * half, :] = part[c * half : (c + 1) * half]
    for n in range(2):
        part = values[1, :, (1 + n) * HD : (2 + n) * HD].astype(jnp.float32)
        turned[2 + n] = jnp.transpose(part)
    for j in range(4):
        g = group if j % 2 == 0 else 1 - group
        c = core if j // 2 == 0 else 1 - core
        block = turned[jnp.where(g == 0, c, 2 + j // 2)]
        vg[:, j * rows : (j + 1) * rows] = block.astype(vg.dtype)
    chips, stripes, depth, span = out.shape
    span = span // 2
    for t in range(0, stripes, 2):
        part = slice(t * span, (t + 2) * span)
        x = jnp.concatenate(
            [mine[:, part], across[:, part], beside[:, part], corner[:, part]], axis=0
        )
        block = product(vg[...], x, 0)
        for n in range(2):
            piece = block[:, n * span : (n + 1) * span].reshape(chips, 2, depth, span)
            piece = jnp.concatenate([piece[:, 0], piece[:, 1]], axis=-1)
            out[:, t + n] = piece.astype(out.dtype)


def fold_kernel(owners, pieces, out, total):
    acc = pieces[0].astype(jnp.float32)
    for i in range(1, pieces.shape[0]):
        acc = acc + pieces[i].astype(jnp.float32)
    total[...] = acc
    half = total.shape[1] // 2
    span = half // owners
    out[...] = jnp.zeros(out.shape, out.dtype)
    for r in range(owners):
        out[r, :, :span] = total[:, r * span : (r + 1) * span]
        out[r, :, 64 : 64 + span] = total[:, half + r * span : half + (r + 1) * span]


def adam_kernel(scale, pieces, m, v, new_m, new_v, update):
    acc = pieces[0]
    for i in range(1, pieces.shape[0]):
        acc = acc + pieces[i]
    span = m.shape[1]
    gradient = jnp.concatenate([acc[:, :span], acc[:, 64 : 64 + span]], axis=0) * scale
    first = 0.9 * m[...] + 0.1 * gradient
    second = 0.95 * v[...] + 0.05 * gradient * gradient
    new_m[...] = first
    new_v[...] = second
    update[...] = first / (1.0 - 0.9**STEP) / (jnp.sqrt(second / (1.0 - 0.95**STEP)) + 1e-08)


def call(kernel, out, scalars, arrays, scratch=(), flops=0):
    many = isinstance(out, tuple)
    return pl.pallas_call(
        kernel,
        out_shape=out,
        in_specs=[SCALARS] * len(scalars) + [WHOLE] * len(arrays),
        out_specs=(WHOLE,) * len(out) if many else WHOLE,
        scratch_shapes=list(scratch),
        compiler_params=PARAMS,
        cost_estimate=pl.CostEstimate(flops=flops, bytes_accessed=0, transcendentals=0),
    )(*scalars, *arrays)


def body(layer_input, queries, keys, d_out, doc_start, moment_m, moment_v):
    rows = queries.shape[1]
    chips, cores = lax.axis_size("x"), lax.axis_size("core")
    stripes, owners = lax.axis_size("yh"), lax.axis_size("z")
    blocks = chips * cores
    seq = blocks * rows
    width, cols = layer_input.shape[2], KV_HEADS * HD
    half, share = width // 2, cols // blocks
    heads = GROUP * HD
    bf16, f32 = jnp.bfloat16, jnp.float32
    shape = jax.ShapeDtypeStruct

    group, core = lax.axis_index("grp"), lax.axis_index("core")
    index = lax.axis_index("x") * cores + core
    first_row = index * rows
    place = jnp.stack([group, first_row, first_row // CHUNK, index, core]).astype(jnp.int32)
    q, d, k = queries[0], d_out[0], keys[0]

    down, swap = [(0, 1)], [(0, 1), (1, 0)]
    other_k = lax.ppermute(k, "grp", down)
    other = lax.ppermute(jnp.concatenate([q[:, heads:], d[:, heads:]], axis=1), "grp", down)
    lower, upper = layer_input[0, :, :half], layer_input[0, :, half:]
    mine = jnp.where(group == 0, lower, upper)
    theirs = jnp.where(group == 0, upper, lower)
    across = lax.ppermute(theirs, "grp", swap)
    chosen = jnp.where(group == 0, k[:, :HD], other_k[:, HD:])
    all_keys = lax.all_gather(chosen, ("x", "core"), axis=0, tiled=True)
    partial = call(
        functools.partial(long_kernel, share),
        shape((seq, HD), bf16),
        [place],
        [q, d, other, all_keys],
        [
            pltpu.VMEM((heads, HD), bf16),
            pltpu.VMEM((heads, HD), bf16),
            pltpu.VMEM((seq, GROUP * rows), f32),
        ],
        flops=6 * 10**9,
    )
    partial, across, mine, begin = lax.optimization_barrier((partial, across, mine, doc_start))
    square = shape((rows, HD), bf16)
    stay, leave = call(
        functools.partial(local_kernel, share),
        (square, square),
        [place],
        [begin, q, d, k],
        [pltpu.VMEM((heads, HD), bf16), pltpu.VMEM((heads, HD), bf16)],
        flops=3 * 10**9,
    )
    beside = lax.ppermute(mine, "core", swap)
    corner = lax.ppermute(across, "core", swap)
    got = lax.ppermute(leave, "core", swap)
    pieces = lax.all_to_all(
        partial.reshape(blocks, rows, HD), ("x", "core"), 0, 0, tiled=True
    )
    values = call(value_kernel, shape((rows, 3 * HD), bf16), [], [pieces, stay, got])
    values = lax.all_gather(values, "grp", axis=0)
    gradient = call(
        project_kernel,
        shape((chips, stripes, share // 2, 2 * half // stripes), bf16),
        [place],
        [values, mine, across, beside, corner],
        [pltpu.VMEM((4, cols // 2, rows), f32), pltpu.VMEM((cols // 2, 4 * rows), bf16)],
    )
    gradient = gradient.reshape(chips * stripes, share // 2, 2 * half // stripes)
    terms = lax.all_to_all(gradient, ("x", "yh"), 0, 0, tiled=True)
    sent = call(
        functools.partial(fold_kernel, owners),
        shape((owners, 8, 128), f32),
        [],
        [terms],
        [pltpu.VMEM((share // 2, 2 * half // stripes), f32)],
    )
    landed = lax.all_to_all(sent, "z", 0, 0, tiled=True)
    result = shape(moment_m.shape[::-1], f32)
    total_tokens = 2 * stripes * owners * seq
    outs = call(
        functools.partial(adam_kernel, 1.0 / math.sqrt(total_tokens)),
        (result,) * 3,
        [],
        [landed, moment_m.T, moment_v.T],
    )
    return tuple(o.T for o in outs)


def solution(mesh):
    groups, copies, blocks = mesh.devices.shape
    split = mesh.devices.reshape(groups, 4, copies // 4, blocks // 2, 2)
    mesh = Mesh(split, ("grp", "yh", "z", "x", "core"))
    slots, tokens = ("grp", "yh", "z"), ("x", "core")
    wide, flat = P(slots, tokens, None), P(slots, tokens)
    in_specs = (wide, wide, wide, wide, flat, flat, flat)
    return jax.shard_map(
        body, mesh=mesh, in_specs=in_specs, out_specs=(flat,) * 3, check_vma=False
    )
```

```python
import functools
import math

import jax
import jax.numpy as jnp
from jax import lax
from jax.experimental import pallas as pl
from jax.experimental.pallas import tpu as pltpu
from jax.sharding import Mesh
from jax.sharding import PartitionSpec as P

KV_HEADS = 2
HD = 128
STEP = 10
GROUP = 7
CHUNK = 512
masked_score = -1e30
GAIN = HD ** (-0.5) * math.log2(math.e)
WHOLE = pl.BlockSpec(memory_space=pltpu.VMEM)
SCALARS = pl.BlockSpec(memory_space=pltpu.SMEM)
PARAMS = pltpu.CompilerParams(vmem_limit_bytes=24 * 1024 * 1024)


def product(a, b, axis):
    return lax.dot_general(
        a, b, (((1,), (axis,)), ((), ())), preferred_element_type=jnp.float32
    )


def lanes_of_queries(row):
    return jnp.concatenate([row] * GROUP, axis=1)


def by_parity(matrix, share):
    width = matrix.shape[1]
    old = lax.broadcasted_iota(jnp.int32, (width, width), 0)
    new = lax.broadcasted_iota(jnp.int32, (width, width), 1)
    half = width // 2
    within = new % half
    source = (2 * (within // share) + new // half) * share + within % share
    chosen = jnp.where(old == source, 1.0, 0.0).astype(matrix.dtype)
    return product(matrix, chosen, 0).astype(matrix.dtype)


def join(a, b, parity):
    half = a.shape[1] // 2
    part = slice(parity * half, (parity + 1) * half)
    return jnp.concatenate([a[:, part], b[:, part]], axis=1)


def local_kernel(share, place, begin, q, d, k, stay, leave, qs, ds):
    rows = q.shape[0]
    width = GROUP * rows

    @pl.when(place[0] == 0)
    def _():
        stay[...] = jnp.zeros(stay.shape, stay.dtype)
        leave[...] = jnp.zeros(leave.shape, leave.dtype)

    @pl.when(place[0] == 1)
    def _():
        first = lanes_of_queries(begin[...] - place[1])
        query_pos = lanes_of_queries(lax.broadcasted_iota(jnp.int32, (1, rows), 1))
        key_pos = lax.broadcasted_iota(jnp.int32, (rows, width), 0)
        visible = (key_pos >= first) & (key_pos <= query_pos)
        sums = []
        for g in range(KV_HEADS):
            for r in range(GROUP):
                h = g * GROUP + r
                qs[r * rows : (r + 1) * rows, :] = q[:, h * HD : (h + 1) * HD]
                ds[r * rows : (r + 1) * rows, :] = d[:, h * HD : (h + 1) * HD]
            cols = slice(g * HD, (g + 1) * HD)
            x = jnp.where(visible, product(k[:, cols], qs[...], 1) * GAIN, masked_score)
            top = jnp.max(x, axis=0, keepdims=True)
            shift = top + jnp.log2(jnp.sum(jnp.exp2(x - top), axis=0, keepdims=True))
            p = jnp.exp2(x - shift).astype(ds.dtype)
            sums.append(product(p, by_parity(ds[...], share), 0))
        even, odd = (join(*sums, parity).astype(stay.dtype) for parity in range(2))
        stay[...] = jnp.where(place[4] == 0, even, odd)
        leave[...] = jnp.where(place[4] == 0, odd, even)


def long_kernel(share, place, q, d, other, k, out, qs, ds, s):
    seq, rows = k.shape[0], q.shape[0]
    width = GROUP * rows
    first_row, high = place[1], place[2]

    @pl.when(place[0] == 0)
    def _():
        for r in range(GROUP):
            qs[r * rows : (r + 1) * rows, :] = q[:, r * HD : (r + 1) * HD]
            ds[r * rows : (r + 1) * rows, :] = d[:, r * HD : (r + 1) * HD]

    @pl.when(place[0] == 1)
    def _():
        for r in range(GROUP):
            h = GROUP + r
            qs[r * rows : (r + 1) * rows, :] = other[:, r * HD : (r + 1) * HD]
            ds[r * rows : (r + 1) * rows, :] = other[:, h * HD : (h + 1) * HD]

    ds[...] = by_parity(ds[...], share)

    def chunk_rows(c):
        return pl.ds(pl.multiple_of(c * CHUNK, CHUNK), CHUNK)

    def clear(c, carry):
        out[chunk_rows(c), :] = jnp.zeros((CHUNK, HD), out.dtype)
        return carry

    lax.fori_loop(high + 1, seq // CHUNK, clear, 0)

    def absorb(x, top, total):
        x = x.reshape(CHUNK // 8, 8, width)
        larger = jnp.maximum(top, jnp.max(x, axis=0))
        total = total * jnp.exp2(top - larger) + jnp.sum(jnp.exp2(x - larger), axis=0)
        return larger, total

    def inner(c, carry):
        x = product(k[chunk_rows(c), :], qs[...], 1) * GAIN
        s[chunk_rows(c), :] = x
        return absorb(x, *carry)

    empty = jnp.full((8, width), masked_score, jnp.float32), jnp.zeros((8, width), jnp.float32)
    top, total = lax.fori_loop(0, high, inner, empty)
    query_pos = first_row + lanes_of_queries(lax.broadcasted_iota(jnp.int32, (1, rows), 1))
    key_pos = high * CHUNK + lax.broadcasted_iota(jnp.int32, (CHUNK, width), 0)
    x = product(k[chunk_rows(high), :], qs[...], 1) * GAIN
    x = jnp.where(key_pos <= query_pos, x, masked_score)
    s[chunk_rows(high), :] = x
    top, total = absorb(x, top, total)
    most = jnp.max(top, axis=0, keepdims=True)
    total = jnp.sum(total * jnp.exp2(top - most), axis=0, keepdims=True)
    shift = most + jnp.log2(total)

    def collect(c, carry):
        p = jnp.exp2(s[chunk_rows(c), :] - shift).astype(ds.dtype)
        block = product(p, ds[...], 0)
        for i in range(0, CHUNK // rows, 2):
            pair = [block[(i + n) * rows : (i + n + 1) * rows] for n in range(2)]
            for parity in range(2):
                at = pl.ds(pl.multiple_of(c * CHUNK + (i + parity) * rows, rows), rows)
                out[at, :] = join(*pair, parity).astype(out.dtype)
        return carry

    lax.fori_loop(0, high + 1, collect, 0)


def value_kernel(pieces, out):
    total = pieces[0].astype(jnp.float32)
    for i in range(1, pieces.shape[0]):
        total = total + pieces[i].astype(jnp.float32)
    out[...] = total.astype(out.dtype)


def project_kernel(
    place, values, stay, got, near, far, mine, across, beside, corner, out, turned, vg
):
    rows = values.shape[1]
    group, core = place[0], place[4]
    half = HD // 2
    for g in range(KV_HEADS):
        part = jnp.transpose(values[g, :, :HD].astype(jnp.float32))
        for c in range(2):
            turned[c, g * half : (g + 1) * half, :] = part[c * half : (c + 1) * half]
    for n, (here, sent) in enumerate(((stay, near), (got, far))):
        part = jnp.where(group == 1, here[...].astype(jnp.float32), sent[...].astype(jnp.float32))
        turned[2 + n] = jnp.transpose(part)
    for j in range(4):
        g = group if j % 2 == 0 else 1 - group
        c = core if j // 2 == 0 else 1 - core
        block = turned[jnp.where(g == 0, c, 2 + j // 2)]
        vg[:, j * rows : (j + 1) * rows] = block.astype(vg.dtype)
    chips, stripes, depth, span = out.shape
    span = span // 2
    for t in range(0, stripes, 2):
        part = slice(t * span, (t + 2) * span)
        x = jnp.concatenate(
            [mine[:, part], across[:, part], beside[:, part], corner[:, part]], axis=0
        )
        block = product(vg[...], x, 0)
        for n in range(2):
            piece = block[:, n * span : (n + 1) * span].reshape(chips, 2, depth, span)
            piece = jnp.concatenate([piece[:, 0], piece[:, 1]], axis=-1)
            out[:, t + n] = piece.astype(out.dtype)


def fold_kernel(owners, pieces, out, total):
    acc = pieces[0].astype(jnp.float32)
    for i in range(1, pieces.shape[0]):
        acc = acc + pieces[i].astype(jnp.float32)
    total[...] = acc
    half = total.shape[1] // 2
    span = half // owners
    out[...] = jnp.zeros(out.shape, out.dtype)
    for r in range(owners):
        out[r, :, :span] = total[:, r * span : (r + 1) * span]
        out[r, :, 64 : 64 + span] = total[:, half + r * span : half + (r + 1) * span]


def adam_kernel(scale, pieces, m, v, new_m, new_v, update):
    acc = pieces[0]
    for i in range(1, pieces.shape[0]):
        acc = acc + pieces[i]
    span = m.shape[1]
    gradient = jnp.concatenate([acc[:, :span], acc[:, 64 : 64 + span]], axis=0) * scale
    first = 0.9 * m[...] + 0.1 * gradient
    second = 0.95 * v[...] + 0.05 * gradient * gradient
    new_m[...] = first
    new_v[...] = second
    update[...] = first / (1.0 - 0.9**STEP) / (jnp.sqrt(second / (1.0 - 0.95**STEP)) + 1e-08)


def call(kernel, out, scalars, arrays, scratch=(), flops=0):
    many = isinstance(out, tuple)
    return pl.pallas_call(
        kernel,
        out_shape=out,
        in_specs=[SCALARS] * len(scalars) + [WHOLE] * len(arrays),
        out_specs=(WHOLE,) * len(out) if many else WHOLE,
        scratch_shapes=list(scratch),
        compiler_params=PARAMS,
        cost_estimate=pl.CostEstimate(flops=flops, bytes_accessed=0, transcendentals=0),
    )(*scalars, *arrays)


def body(layer_input, queries, keys, d_out, doc_start, moment_m, moment_v):
    rows = queries.shape[1]
    chips, cores = lax.axis_size("x"), lax.axis_size("core")
    stripes, owners = lax.axis_size("yh"), lax.axis_size("z")
    blocks = chips * cores
    seq = blocks * rows
    width, cols = layer_input.shape[2], KV_HEADS * HD
    half, share = width // 2, cols // blocks
    heads = GROUP * HD
    bf16, f32 = jnp.bfloat16, jnp.float32
    shape = jax.ShapeDtypeStruct

    group, core = lax.axis_index("grp"), lax.axis_index("core")
    index = lax.axis_index("x") * cores + core
    first_row = index * rows
    place = jnp.stack([group, first_row, first_row // CHUNK, index, core]).astype(jnp.int32)
    q, d, k = queries[0], d_out[0], keys[0]

    down, swap = [(0, 1)], [(0, 1), (1, 0)]
    other_k = lax.ppermute(k, "grp", down)
    other = lax.ppermute(jnp.concatenate([q[:, heads:], d[:, heads:]], axis=1), "grp", down)
    lower, upper = layer_input[0, :, :half], layer_input[0, :, half:]
    mine = jnp.where(group == 0, lower, upper)
    theirs = jnp.where(group == 0, upper, lower)
    across = lax.ppermute(theirs, "grp", swap)
    chosen = jnp.where(group == 0, k[:, :HD], other_k[:, HD:])
    all_keys = lax.all_gather(chosen, ("x", "core"), axis=0, tiled=True)
    partial = call(
        functools.partial(long_kernel, share),
        shape((seq, HD), bf16),
        [place],
        [q, d, other, all_keys],
        [
            pltpu.VMEM((heads, HD), bf16),
            pltpu.VMEM((heads, HD), bf16),
            pltpu.VMEM((seq, GROUP * rows), f32),
        ],
        flops=6 * 10**9,
    )
    partial, across, mine, begin = lax.optimization_barrier((partial, across, mine, doc_start))
    square = shape((rows, HD), bf16)
    stay, leave = call(
        functools.partial(local_kernel, share),
        (square, square),
        [place],
        [begin, q, d, k],
        [pltpu.VMEM((heads, HD), bf16), pltpu.VMEM((heads, HD), bf16)],
        flops=3 * 10**9,
    )
    beside = lax.ppermute(mine, "core", swap)
    corner = lax.ppermute(across, "core", swap)
    got = lax.ppermute(leave, "core", swap)
    near = lax.ppermute(stay, "grp", [(1, 0)])
    far = lax.ppermute(leave, ("grp", "core"), [(2, 1), (3, 0)])
    pieces = lax.all_to_all(
        partial.reshape(blocks, rows, HD), ("x", "core"), 0, 0, tiled=True
    )
    values = call(value_kernel, square, [], [pieces])
    values = lax.all_gather(values, "grp", axis=0)
    gradient = call(
        project_kernel,
        shape((chips, stripes, share // 2, 2 * half // stripes), bf16),
        [place],
        [values, stay, got, near, far, mine, across, beside, corner],
        [pltpu.VMEM((4, cols // 2, rows), f32), pltpu.VMEM((cols // 2, 4 * rows), bf16)],
    )
    gradient = gradient.reshape(chips * stripes, share // 2, 2 * half // stripes)
    terms = lax.all_to_all(gradient, ("x", "yh"), 0, 0, tiled=True)
    sent = call(
        functools.partial(fold_kernel, owners),
        shape((owners, 8, 128), f32),
        [],
        [terms],
        [pltpu.VMEM((share // 2, 2 * half // stripes), f32)],
    )
    landed = lax.all_to_all(sent, "z", 0, 0, tiled=True)
    result = shape(moment_m.shape[::-1], f32)
    total_tokens = 2 * stripes * owners * seq
    outs = call(
        functools.partial(adam_kernel, 1.0 / math.sqrt(total_tokens)),
        (result,) * 3,
        [],
        [landed, moment_m.T, moment_v.T],
    )
    return tuple(o.T for o in outs)


def solution(mesh):
    groups, copies, blocks = mesh.devices.shape
    split = mesh.devices.reshape(groups, 4, copies // 4, blocks // 2, 2)
    mesh = Mesh(split, ("grp", "yh", "z", "x", "core"))
    slots, tokens = ("grp", "yh", "z"), ("x", "core")
    wide, flat = P(slots, tokens, None), P(slots, tokens)
    in_specs = (wide, wide, wide, wide, flat, flat, flat)
    return jax.shard_map(
        body, mesh=mesh, in_specs=in_specs, out_specs=(flat,) * 3, check_vma=False
    )
```

```python
import functools
import math

import jax
import jax.numpy as jnp
from jax import lax
from jax.experimental import pallas as pl
from jax.experimental.pallas import tpu as pltpu
from jax.sharding import Mesh
from jax.sharding import PartitionSpec as P

KV_HEADS = 2
HD = 128
STEP = 10
GROUP = 7
CHUNK = 512
masked_score = -1e30
GAIN = HD ** (-0.5) * math.log2(math.e)
WHOLE = pl.BlockSpec(memory_space=pltpu.VMEM)
SCALARS = pl.BlockSpec(memory_space=pltpu.SMEM)
PARAMS = pltpu.CompilerParams(vmem_limit_bytes=24 * 1024 * 1024)


def product(a, b, axis):
    return lax.dot_general(
        a, b, (((1,), (axis,)), ((), ())), preferred_element_type=jnp.float32
    )


def lanes_of_queries(row):
    return jnp.concatenate([row] * GROUP, axis=1)


def by_parity(matrix, share):
    width = matrix.shape[1]
    old = lax.broadcasted_iota(jnp.int32, (width, width), 0)
    new = lax.broadcasted_iota(jnp.int32, (width, width), 1)
    half = width // 2
    within = new % half
    source = (2 * (within // share) + new // half) * share + within % share
    chosen = jnp.where(old == source, 1.0, 0.0).astype(matrix.dtype)
    return product(matrix, chosen, 0).astype(matrix.dtype)


def join(a, b, parity):
    half = a.shape[1] // 2
    part = slice(parity * half, (parity + 1) * half)
    return jnp.concatenate([a[:, part], b[:, part]], axis=1)


def local_kernel(share, place, begin, q, d, k, stay, leave, qs, ds):
    rows = q.shape[0]
    width = GROUP * rows

    @pl.when(place[0] == 0)
    def _():
        stay[...] = jnp.zeros(stay.shape, stay.dtype)
        leave[...] = jnp.zeros(leave.shape, leave.dtype)

    @pl.when(place[0] == 1)
    def _():
        first = lanes_of_queries(begin[...] - place[1])
        query_pos = lanes_of_queries(lax.broadcasted_iota(jnp.int32, (1, rows), 1))
        key_pos = lax.broadcasted_iota(jnp.int32, (rows, width), 0)
        visible = (key_pos >= first) & (key_pos <= query_pos)
        sums = []
        for g in range(KV_HEADS):
            for r in range(GROUP):
                h = g * GROUP + r
                qs[r * rows : (r + 1) * rows, :] = q[:, h * HD : (h + 1) * HD]
                ds[r * rows : (r + 1) * rows, :] = d[:, h * HD : (h + 1) * HD]
            cols = slice(g * HD, (g + 1) * HD)
            x = jnp.where(visible, product(k[:, cols], qs[...], 1) * GAIN, masked_score)
            top = jnp.max(x, axis=0, keepdims=True)
            shift = top + jnp.log2(jnp.sum(jnp.exp2(x - top), axis=0, keepdims=True))
            p = jnp.exp2(x - shift).astype(ds.dtype)
            sums.append(product(p, by_parity(ds[...], share), 0))
        even, odd = (join(*sums, parity).astype(stay.dtype) for parity in range(2))
        stay[...] = jnp.where(place[4] == 0, even, odd)
        leave[...] = jnp.where(place[4] == 0, odd, even)


def long_kernel(share, place, q, d, other, k, out, qs, ds, s):
    seq, rows = k.shape[0], q.shape[0]
    width = GROUP * rows
    first_row, high = place[1], place[2]

    @pl.when(place[0] == 0)
    def _():
        for r in range(GROUP):
            qs[r * rows : (r + 1) * rows, :] = q[:, r * HD : (r + 1) * HD]
            ds[r * rows : (r + 1) * rows, :] = d[:, r * HD : (r + 1) * HD]

    @pl.when(place[0] == 1)
    def _():
        for r in range(GROUP):
            h = GROUP + r
            qs[r * rows : (r + 1) * rows, :] = other[:, r * HD : (r + 1) * HD]
            ds[r * rows : (r + 1) * rows, :] = other[:, h * HD : (h + 1) * HD]

    ds[...] = by_parity(ds[...], share)

    def chunk_rows(c):
        return pl.ds(pl.multiple_of(c * CHUNK, CHUNK), CHUNK)

    def piece_rows(c, parity, n, count):
        start = parity * (seq // 2) + c * (CHUNK // 2) + n * rows
        return pl.ds(pl.multiple_of(start, rows), count * rows)

    def clear(c, carry):
        for parity in range(2):
            at = piece_rows(c, parity, 0, CHUNK // rows // 2)
            out[at, :] = jnp.zeros((CHUNK // 2, HD), out.dtype)
        return carry

    lax.fori_loop(high + 1, seq // CHUNK, clear, 0)

    def absorb(x, top, total):
        x = x.reshape(CHUNK // 8, 8, width)
        larger = jnp.maximum(top, jnp.max(x, axis=0))
        total = total * jnp.exp2(top - larger) + jnp.sum(jnp.exp2(x - larger), axis=0)
        return larger, total

    def inner(c, carry):
        x = product(k[chunk_rows(c), :], qs[...], 1) * GAIN
        s[chunk_rows(c), :] = x
        return absorb(x, *carry)

    empty = jnp.full((8, width), masked_score, jnp.float32), jnp.zeros((8, width), jnp.float32)
    top, total = lax.fori_loop(0, high, inner, empty)
    query_pos = first_row + lanes_of_queries(lax.broadcasted_iota(jnp.int32, (1, rows), 1))
    key_pos = high * CHUNK + lax.broadcasted_iota(jnp.int32, (CHUNK, width), 0)
    x = product(k[chunk_rows(high), :], qs[...], 1) * GAIN
    x = jnp.where(key_pos <= query_pos, x, masked_score)
    s[chunk_rows(high), :] = x
    top, total = absorb(x, top, total)
    most = jnp.max(top, axis=0, keepdims=True)
    total = jnp.sum(total * jnp.exp2(top - most), axis=0, keepdims=True)
    shift = most + jnp.log2(total)

    def collect(c, carry):
        p = jnp.exp2(s[chunk_rows(c), :] - shift).astype(ds.dtype)
        block = product(p, ds[...], 0)
        for i in range(0, CHUNK // rows, 2):
            pair = [block[(i + n) * rows : (i + n + 1) * rows] for n in range(2)]
            for parity in range(2):
                at = piece_rows(c, parity, i // 2, 1)
                out[at, :] = join(*pair, parity).astype(out.dtype)
        return carry

    lax.fori_loop(0, high + 1, collect, 0)


def value_kernel(pieces, out):
    total = pieces[0].astype(jnp.float32)
    for i in range(1, pieces.shape[0]):
        total = total + pieces[i].astype(jnp.float32)
    out[...] = total.astype(out.dtype)


def project_kernel(
    place, values, stay, got, near, far, mine, across, beside, corner, out, turned, vg
):
    rows = values.shape[1]
    group, core = place[0], place[4]
    half = HD // 2
    for g in range(KV_HEADS):
        part = jnp.transpose(values[g, :, :HD].astype(jnp.float32))
        for c in range(2):
            turned[c, g * half : (g + 1) * half, :] = part[c * half : (c + 1) * half]
    for n, (here, sent) in enumerate(((stay, near), (got, far))):
        part = jnp.where(group == 1, here[...].astype(jnp.float32), sent[...].astype(jnp.float32))
        turned[2 + n] = jnp.transpose(part)
    for j in range(4):
        g = group if j % 2 == 0 else 1 - group
        c = core if j // 2 == 0 else 1 - core
        block = turned[jnp.where(g == 0, c, 2 + j // 2)]
        vg[:, j * rows : (j + 1) * rows] = block.astype(vg.dtype)
    stripes, chips, depth, span = out.shape
    span = span // 2
    for t in range(0, stripes, 2):
        part = slice(t * span, (t + 2) * span)
        x = jnp.concatenate(
            [mine[:, part], across[:, part], beside[:, part], corner[:, part]], axis=0
        )
        block = product(vg[...], x, 0)
        for n in range(2):
            piece = block[:, n * span : (n + 1) * span].reshape(chips, 2, depth, span)
            piece = jnp.concatenate([piece[:, 0], piece[:, 1]], axis=-1)
            out[t + n] = piece.astype(out.dtype)


def fold_kernel(owners, pieces, out, total):
    acc = pieces[0].astype(jnp.float32)
    for i in range(1, pieces.shape[0]):
        acc = acc + pieces[i].astype(jnp.float32)
    total[...] = acc
    half = total.shape[1] // 2
    span = half // owners
    out[...] = jnp.zeros(out.shape, out.dtype)
    for r in range(owners):
        out[r, :, :span] = total[:, r * span : (r + 1) * span]
        out[r, :, 64 : 64 + span] = total[:, half + r * span : half + (r + 1) * span]


def adam_kernel(scale, pieces, m, v, new_m, new_v, update):
    acc = pieces[0]
    for i in range(1, pieces.shape[0]):
        acc = acc + pieces[i]
    span = m.shape[1]
    gradient = jnp.concatenate([acc[:, :span], acc[:, 64 : 64 + span]], axis=0) * scale
    first = 0.9 * m[...] + 0.1 * gradient
    second = 0.95 * v[...] + 0.05 * gradient * gradient
    new_m[...] = first
    new_v[...] = second
    update[...] = first / (1.0 - 0.9**STEP) / (jnp.sqrt(second / (1.0 - 0.95**STEP)) + 1e-08)


def call(kernel, out, scalars, arrays, scratch=(), flops=0):
    many = isinstance(out, tuple)
    return pl.pallas_call(
        kernel,
        out_shape=out,
        in_specs=[SCALARS] * len(scalars) + [WHOLE] * len(arrays),
        out_specs=(WHOLE,) * len(out) if many else WHOLE,
        scratch_shapes=list(scratch),
        compiler_params=PARAMS,
        cost_estimate=pl.CostEstimate(flops=flops, bytes_accessed=0, transcendentals=0),
    )(*scalars, *arrays)


def body(layer_input, queries, keys, d_out, doc_start, moment_m, moment_v):
    rows = queries.shape[1]
    chips, cores = lax.axis_size("x"), lax.axis_size("core")
    stripes, owners = lax.axis_size("yh"), lax.axis_size("z")
    blocks = chips * cores
    seq = blocks * rows
    width, cols = layer_input.shape[2], KV_HEADS * HD
    half, share = width // 2, cols // blocks
    heads = GROUP * HD
    bf16, f32 = jnp.bfloat16, jnp.float32
    shape = jax.ShapeDtypeStruct

    group, core = lax.axis_index("grp"), lax.axis_index("core")
    index = lax.axis_index("x") * cores + core
    first_row = index * rows
    place = jnp.stack([group, first_row, first_row // CHUNK, index, core]).astype(jnp.int32)
    q, d, k = queries[0], d_out[0], keys[0]

    down, swap = [(0, 1)], [(0, 1), (1, 0)]
    other_k = lax.ppermute(k, "grp", down)
    other = lax.ppermute(jnp.concatenate([q[:, heads:], d[:, heads:]], axis=1), "grp", down)
    lower, upper = layer_input[0, :, :half], layer_input[0, :, half:]
    mine = jnp.where(group == 0, lower, upper)
    theirs = jnp.where(group == 0, upper, lower)
    across = lax.ppermute(theirs, "grp", swap)
    chosen = jnp.where(group == 0, k[:, :HD], other_k[:, HD:])
    all_keys = lax.all_gather(chosen, ("x", "core"), axis=0, tiled=True)
    partial = call(
        functools.partial(long_kernel, share),
        shape((seq, HD), bf16),
        [place],
        [q, d, other, all_keys],
        [
            pltpu.VMEM((heads, HD), bf16),
            pltpu.VMEM((heads, HD), bf16),
            pltpu.VMEM((seq, GROUP * rows), f32),
        ],
        flops=6 * 10**9,
    )
    partial, across, mine, begin = lax.optimization_barrier((partial, across, mine, doc_start))
    square = shape((rows, HD), bf16)
    stay, leave = call(
        functools.partial(local_kernel, share),
        (square, square),
        [place],
        [begin, q, d, k],
        [pltpu.VMEM((heads, HD), bf16), pltpu.VMEM((heads, HD), bf16)],
        flops=3 * 10**9,
    )
    beside = lax.ppermute(mine, "core", swap)
    corner = lax.ppermute(across, "core", swap)
    got = lax.ppermute(leave, "core", swap)
    near = lax.ppermute(stay, "grp", [(1, 0)])
    far = lax.ppermute(leave, ("grp", "core"), [(2, 1), (3, 0)])
    pieces = lax.all_to_all(
        partial.reshape(blocks, rows, HD), ("core", "x"), 0, 0, tiled=True
    )
    values = call(value_kernel, square, [], [pieces])
    values = lax.all_gather(values, "grp", axis=0)
    gradient = call(
        project_kernel,
        shape((stripes, chips, share // 2, 2 * half // stripes), bf16),
        [place],
        [values, stay, got, near, far, mine, across, beside, corner],
        [pltpu.VMEM((4, cols // 2, rows), f32), pltpu.VMEM((cols // 2, 4 * rows), bf16)],
    )
    gradient = gradient.reshape(chips * stripes, share // 2, 2 * half // stripes)
    terms = lax.all_to_all(gradient, ("yh", "x"), 0, 0, tiled=True)
    sent = call(
        functools.partial(fold_kernel, owners),
        shape((owners, 8, 128), f32),
        [],
        [terms],
        [pltpu.VMEM((share // 2, 2 * half // stripes), f32)],
    )
    landed = lax.all_to_all(sent, "z", 0, 0, tiled=True)
    result = shape(moment_m.shape[::-1], f32)
    total_tokens = 2 * stripes * owners * seq
    outs = call(
        functools.partial(adam_kernel, 1.0 / math.sqrt(total_tokens)),
        (result,) * 3,
        [],
        [landed, moment_m.T, moment_v.T],
    )
    return tuple(o.T for o in outs)


def solution(mesh):
    groups, copies, blocks = mesh.devices.shape
    split = mesh.devices.reshape(groups, 4, copies // 4, blocks // 2, 2)
    mesh = Mesh(split, ("grp", "yh", "z", "x", "core"))
    slots, tokens = ("grp", "yh", "z"), ("x", "core")
    wide, flat = P(slots, tokens, None), P(slots, tokens)
    in_specs = (wide, wide, wide, wide, flat, flat, flat)
    return jax.shard_map(
        body, mesh=mesh, in_specs=in_specs, out_specs=(flat,) * 3, check_vma=False
    )
```

```python
import functools
import math

import jax
import jax.numpy as jnp
from jax import lax
from jax.experimental import pallas as pl
from jax.experimental.pallas import tpu as pltpu
from jax.sharding import Mesh
from jax.sharding import PartitionSpec as P

KV_HEADS = 2
HD = 128
STEP = 10
GROUP = 7
CHUNK = 512
masked_score = -1e30
GAIN = HD ** (-0.5) * math.log2(math.e)
WHOLE = pl.BlockSpec(memory_space=pltpu.VMEM)
SCALARS = pl.BlockSpec(memory_space=pltpu.SMEM)
PARAMS = pltpu.CompilerParams(vmem_limit_bytes=24 * 1024 * 1024)


def product(a, b, axis):
    return lax.dot_general(
        a, b, (((1,), (axis,)), ((), ())), preferred_element_type=jnp.float32
    )


def lanes_of_queries(row):
    return jnp.concatenate([row] * GROUP, axis=1)


def by_parity(matrix, share):
    width = matrix.shape[1]
    old = lax.broadcasted_iota(jnp.int32, (width, width), 0)
    new = lax.broadcasted_iota(jnp.int32, (width, width), 1)
    half = width // 2
    within = new % half
    source = (2 * (within // share) + new // half) * share + within % share
    chosen = jnp.where(old == source, 1.0, 0.0).astype(matrix.dtype)
    return product(matrix, chosen, 0).astype(matrix.dtype)


def join(a, b, parity):
    half = a.shape[1] // 2
    part = slice(parity * half, (parity + 1) * half)
    return jnp.concatenate([a[:, part], b[:, part]], axis=1)


def local_kernel(share, place, begin, q, d, k, stay, leave, qs, ds):
    rows = q.shape[0]
    width = GROUP * rows

    @pl.when(place[0] == 0)
    def _():
        stay[...] = jnp.zeros(stay.shape, stay.dtype)
        leave[...] = jnp.zeros(leave.shape, leave.dtype)

    @pl.when(place[0] == 1)
    def _():
        first = lanes_of_queries(begin[...] - place[1])
        query_pos = lanes_of_queries(lax.broadcasted_iota(jnp.int32, (1, rows), 1))
        key_pos = lax.broadcasted_iota(jnp.int32, (rows, width), 0)
        visible = (key_pos >= first) & (key_pos <= query_pos)
        sums = []
        for g in range(KV_HEADS):
            for r in range(GROUP):
                h = g * GROUP + r
                qs[r * rows : (r + 1) * rows, :] = q[:, h * HD : (h + 1) * HD]
                ds[r * rows : (r + 1) * rows, :] = d[:, h * HD : (h + 1) * HD]
            cols = slice(g * HD, (g + 1) * HD)
            x = jnp.where(visible, product(k[:, cols], qs[...], 1) * GAIN, masked_score)
            top = jnp.max(x, axis=0, keepdims=True)
            shift = top + jnp.log2(jnp.sum(jnp.exp2(x - top), axis=0, keepdims=True))
            p = jnp.exp2(x - shift).astype(ds.dtype)
            sums.append(product(p, by_parity(ds[...], share), 0))
        even, odd = (join(*sums, parity).astype(stay.dtype) for parity in range(2))
        stay[...] = jnp.where(place[4] == 0, even, odd)
        leave[...] = jnp.where(place[4] == 0, odd, even)


def long_kernel(share, place, q, d, other, k, out, qs, ds, s):
    seq, rows = k.shape[0], q.shape[0]
    width = GROUP * rows
    first_row, high = place[1], place[2]

    @pl.when(place[0] == 0)
    def _():
        for r in range(GROUP):
            qs[r * rows : (r + 1) * rows, :] = q[:, r * HD : (r + 1) * HD]
            ds[r * rows : (r + 1) * rows, :] = d[:, r * HD : (r + 1) * HD]

    @pl.when(place[0] == 1)
    def _():
        for r in range(GROUP):
            h = GROUP + r
            qs[r * rows : (r + 1) * rows, :] = other[:, r * HD : (r + 1) * HD]
            ds[r * rows : (r + 1) * rows, :] = other[:, h * HD : (h + 1) * HD]

    ds[...] = by_parity(ds[...], share)

    def chunk_rows(c):
        return pl.ds(pl.multiple_of(c * CHUNK, CHUNK), CHUNK)

    def clear(c, carry):
        out[chunk_rows(c), :] = jnp.zeros((CHUNK, HD), out.dtype)
        return carry

    lax.fori_loop(high + 1, seq // CHUNK, clear, 0)

    def absorb(x, top, total):
        x = x.reshape(CHUNK // 8, 8, width)
        larger = jnp.maximum(top, jnp.max(x, axis=0))
        total = total * jnp.exp2(top - larger) + jnp.sum(jnp.exp2(x - larger), axis=0)
        return larger, total

    def inner(c, carry):
        x = product(k[chunk_rows(c), :], qs[...], 1) * GAIN
        s[chunk_rows(c), :] = x
        return absorb(x, *carry)

    empty = jnp.full((8, width), masked_score, jnp.float32), jnp.zeros((8, width), jnp.float32)
    top, total = lax.fori_loop(0, high, inner, empty)
    query_pos = first_row + lanes_of_queries(lax.broadcasted_iota(jnp.int32, (1, rows), 1))
    key_pos = high * CHUNK + lax.broadcasted_iota(jnp.int32, (CHUNK, width), 0)
    x = product(k[chunk_rows(high), :], qs[...], 1) * GAIN
    x = jnp.where(key_pos <= query_pos, x, masked_score)
    s[chunk_rows(high), :] = x
    top, total = absorb(x, top, total)
    most = jnp.max(top, axis=0, keepdims=True)
    total = jnp.sum(total * jnp.exp2(top - most), axis=0, keepdims=True)
    shift = most + jnp.log2(total)

    def collect(c, carry):
        p = jnp.exp2(s[chunk_rows(c), :] - shift).astype(ds.dtype)
        block = product(p, ds[...], 0)
        for i in range(0, CHUNK // rows, 2):
            pair = [block[(i + n) * rows : (i + n + 1) * rows] for n in range(2)]
            for parity in range(2):
                at = pl.ds(pl.multiple_of(c * CHUNK + (i + parity) * rows, rows), rows)
                out[at, :] = join(*pair, parity).astype(out.dtype)
        return carry

    lax.fori_loop(0, high + 1, collect, 0)


def value_kernel(pieces, out):
    total = pieces[0].astype(jnp.float32)
    for i in range(1, pieces.shape[0]):
        total = total + pieces[i].astype(jnp.float32)
    out[...] = total.astype(out.dtype)


def project_kernel(
    place, values, stay, got, near, far, mine, across, beside, corner, out, turned, vg
):
    rows = values.shape[1]
    group, core = place[0], place[4]
    half = HD // 2
    for g in range(KV_HEADS):
        part = jnp.transpose(values[g, :, :HD].astype(jnp.float32))
        for c in range(2):
            turned[c, g * half : (g + 1) * half, :] = part[c * half : (c + 1) * half]
    for n, (here, sent) in enumerate(((stay, near), (got, far))):
        part = jnp.where(group == 1, here[...].astype(jnp.float32), sent[...].astype(jnp.float32))
        turned[2 + n] = jnp.transpose(part)
    for j in range(4):
        g = group if j % 2 == 0 else 1 - group
        c = core if j // 2 == 0 else 1 - core
        block = turned[jnp.where(g == 0, c, 2 + j // 2)]
        vg[:, j * rows : (j + 1) * rows] = block.astype(vg.dtype)
    stripes, chips, depth, span = out.shape
    span = span // 2
    for t in range(0, stripes, 2):
        part = slice(t * span, (t + 2) * span)
        x = jnp.concatenate(
            [mine[:, part], across[:, part], beside[:, part], corner[:, part]], axis=0
        )
        block = product(vg[...], x, 0)
        for n in range(2):
            piece = block[:, n * span : (n + 1) * span].reshape(chips, 2, depth, span)
            piece = jnp.concatenate([piece[:, 0], piece[:, 1]], axis=-1)
            out[t + n] = piece.astype(out.dtype)


def fold_kernel(owners, pieces, out, total):
    acc = pieces[0].astype(jnp.float32)
    for i in range(1, pieces.shape[0]):
        acc = acc + pieces[i].astype(jnp.float32)
    total[...] = acc
    half = total.shape[1] // 2
    span = half // owners
    out[...] = jnp.zeros(out.shape, out.dtype)
    for r in range(owners):
        out[r, :, :span] = total[:, r * span : (r + 1) * span]
        out[r, :, 64 : 64 + span] = total[:, half + r * span : half + (r + 1) * span]


def adam_kernel(scale, pieces, m, v, new_m, new_v, update):
    acc = pieces[0]
    for i in range(1, pieces.shape[0]):
        acc = acc + pieces[i]
    span = m.shape[1]
    gradient = jnp.concatenate([acc[:, :span], acc[:, 64 : 64 + span]], axis=0) * scale
    first = 0.9 * m[...] + 0.1 * gradient
    second = 0.95 * v[...] + 0.05 * gradient * gradient
    new_m[...] = first
    new_v[...] = second
    update[...] = first / (1.0 - 0.9**STEP) / (jnp.sqrt(second / (1.0 - 0.95**STEP)) + 1e-08)


def call(kernel, out, scalars, arrays, scratch=(), flops=0):
    many = isinstance(out, tuple)
    return pl.pallas_call(
        kernel,
        out_shape=out,
        in_specs=[SCALARS] * len(scalars) + [WHOLE] * len(arrays),
        out_specs=(WHOLE,) * len(out) if many else WHOLE,
        scratch_shapes=list(scratch),
        compiler_params=PARAMS,
        cost_estimate=pl.CostEstimate(flops=flops, bytes_accessed=0, transcendentals=0),
    )(*scalars, *arrays)


def body(layer_input, queries, keys, d_out, doc_start, moment_m, moment_v):
    rows = queries.shape[1]
    chips, cores = lax.axis_size("x"), lax.axis_size("core")
    stripes, owners = lax.axis_size("yh"), lax.axis_size("z")
    blocks = chips * cores
    seq = blocks * rows
    width, cols = layer_input.shape[2], KV_HEADS * HD
    half, share = width // 2, cols // blocks
    heads = GROUP * HD
    bf16, f32 = jnp.bfloat16, jnp.float32
    shape = jax.ShapeDtypeStruct

    group, core = lax.axis_index("grp"), lax.axis_index("core")
    index = lax.axis_index("x") * cores + core
    first_row = index * rows
    place = jnp.stack([group, first_row, first_row // CHUNK, index, core]).astype(jnp.int32)
    q, d, k = queries[0], d_out[0], keys[0]

    down, swap = [(0, 1)], [(0, 1), (1, 0)]
    other_k = lax.ppermute(k, "grp", down)
    other = lax.ppermute(jnp.concatenate([q[:, heads:], d[:, heads:]], axis=1), "grp", down)
    lower, upper = layer_input[0, :, :half], layer_input[0, :, half:]
    mine = jnp.where(group == 0, lower, upper)
    theirs = jnp.where(group == 0, upper, lower)
    across = lax.ppermute(theirs, "grp", swap)
    chosen = jnp.where(group == 0, k[:, :HD], other_k[:, HD:])
    all_keys = lax.all_gather(chosen, ("x", "core"), axis=0, tiled=True)
    partial = call(
        functools.partial(long_kernel, share),
        shape((seq, HD), bf16),
        [place],
        [q, d, other, all_keys],
        [
            pltpu.VMEM((heads, HD), bf16),
            pltpu.VMEM((heads, HD), bf16),
            pltpu.VMEM((seq, GROUP * rows), f32),
        ],
        flops=6 * 10**9,
    )
    partial, across, mine, begin = lax.optimization_barrier((partial, across, mine, doc_start))
    square = shape((rows, HD), bf16)
    stay, leave = call(
        functools.partial(local_kernel, share),
        (square, square),
        [place],
        [begin, q, d, k],
        [pltpu.VMEM((heads, HD), bf16), pltpu.VMEM((heads, HD), bf16)],
        flops=3 * 10**9,
    )
    beside = lax.ppermute(mine, "core", swap)
    corner = lax.ppermute(across, "core", swap)
    got = lax.ppermute(leave, "core", swap)
    near = lax.ppermute(stay, "grp", [(1, 0)])
    far = lax.ppermute(leave, ("grp", "core"), [(2, 1), (3, 0)])
    pieces = lax.all_to_all(
        partial.reshape(blocks, rows, HD), ("x", "core"), 0, 0, tiled=True
    )
    values = call(value_kernel, square, [], [pieces])
    values = lax.all_gather(values, "grp", axis=0)
    gradient = call(
        project_kernel,
        shape((stripes, chips, share // 2, 2 * half // stripes), bf16),
        [place],
        [values, stay, got, near, far, mine, across, beside, corner],
        [pltpu.VMEM((4, cols // 2, rows), f32), pltpu.VMEM((cols // 2, 4 * rows), bf16)],
    )
    gradient = gradient.reshape(chips * stripes, share // 2, 2 * half // stripes)
    terms = lax.all_to_all(gradient, ("yh", "x"), 0, 0, tiled=True)
    sent = call(
        functools.partial(fold_kernel, owners),
        shape((owners, 8, 128), f32),
        [],
        [terms],
        [pltpu.VMEM((share // 2, 2 * half // stripes), f32)],
    )
    landed = lax.all_to_all(sent, "z", 0, 0, tiled=True)
    result = shape(moment_m.shape[::-1], f32)
    total_tokens = 2 * stripes * owners * seq
    outs = call(
        functools.partial(adam_kernel, 1.0 / math.sqrt(total_tokens)),
        (result,) * 3,
        [],
        [landed, moment_m.T, moment_v.T],
    )
    return tuple(o.T for o in outs)


def solution(mesh):
    groups, copies, blocks = mesh.devices.shape
    split = mesh.devices.reshape(groups, 4, copies // 4, blocks // 2, 2)
    mesh = Mesh(split, ("grp", "yh", "z", "x", "core"))
    slots, tokens = ("grp", "yh", "z"), ("x", "core")
    wide, flat = P(slots, tokens, None), P(slots, tokens)
    in_specs = (wide, wide, wide, wide, flat, flat, flat)
    return jax.shard_map(
        body, mesh=mesh, in_specs=in_specs, out_specs=(flat,) * 3, check_vma=False
    )
```

```python
import functools
import math

import jax
import jax.numpy as jnp
from jax import lax
from jax.experimental import pallas as pl
from jax.experimental.pallas import tpu as pltpu
from jax.sharding import Mesh
from jax.sharding import PartitionSpec as P

KV_HEADS = 2
HD = 128
STEP = 10
GROUP = 7
CHUNK = 512
masked_score = -1e30
GAIN = HD ** (-0.5) * math.log2(math.e)
WHOLE = pl.BlockSpec(memory_space=pltpu.VMEM)
SCALARS = pl.BlockSpec(memory_space=pltpu.SMEM)
PARAMS = pltpu.CompilerParams(vmem_limit_bytes=24 * 1024 * 1024)


def product(a, b, axis):
    return lax.dot_general(
        a, b, (((1,), (axis,)), ((), ())), preferred_element_type=jnp.float32
    )


def lanes_of_queries(row):
    return jnp.concatenate([row] * GROUP, axis=1)


def by_parity(matrix, share):
    width = matrix.shape[1]
    old = lax.broadcasted_iota(jnp.int32, (width, width), 0)
    new = lax.broadcasted_iota(jnp.int32, (width, width), 1)
    half = width // 2
    within = new % half
    source = (2 * (within // share) + new // half) * share + within % share
    chosen = jnp.where(old == source, 1.0, 0.0).astype(matrix.dtype)
    return product(matrix, chosen, 0).astype(matrix.dtype)


def join(a, b, parity):
    half = a.shape[1] // 2
    part = slice(parity * half, (parity + 1) * half)
    return jnp.concatenate([a[:, part], b[:, part]], axis=1)


def local_kernel(share, place, begin, q, d, k, stay, leave, qs, ds):
    rows = q.shape[0]
    width = GROUP * rows

    @pl.when(place[0] == 0)
    def _():
        stay[...] = jnp.zeros(stay.shape, stay.dtype)
        leave[...] = jnp.zeros(leave.shape, leave.dtype)

    @pl.when(place[0] == 1)
    def _():
        first = lanes_of_queries(begin[...] - place[1])
        query_pos = lanes_of_queries(lax.broadcasted_iota(jnp.int32, (1, rows), 1))
        key_pos = lax.broadcasted_iota(jnp.int32, (rows, width), 0)
        visible = (key_pos >= first) & (key_pos <= query_pos)
        sums = []
        for g in range(KV_HEADS):
            for r in range(GROUP):
                h = g * GROUP + r
                qs[r * rows : (r + 1) * rows, :] = q[:, h * HD : (h + 1) * HD]
                ds[r * rows : (r + 1) * rows, :] = d[:, h * HD : (h + 1) * HD]
            cols = slice(g * HD, (g + 1) * HD)
            x = jnp.where(visible, product(k[:, cols], qs[...], 1) * GAIN, masked_score)
            top = jnp.max(x, axis=0, keepdims=True)
            shift = top + jnp.log2(jnp.sum(jnp.exp2(x - top), axis=0, keepdims=True))
            p = jnp.exp2(x - shift).astype(ds.dtype)
            sums.append(product(p, by_parity(ds[...], share), 0))
        even, odd = (join(*sums, parity).astype(stay.dtype) for parity in range(2))
        stay[...] = jnp.where(place[4] == 0, even, odd)
        leave[...] = jnp.where(place[4] == 0, odd, even)


def long_kernel(share, place, q, d, other, k, out, qs, ds, s):
    seq, rows = k.shape[0], q.shape[0]
    width = GROUP * rows
    first_row, high = place[1], place[2]

    @pl.when(place[0] == 0)
    def _():
        for r in range(GROUP):
            qs[r * rows : (r + 1) * rows, :] = q[:, r * HD : (r + 1) * HD]
            ds[r * rows : (r + 1) * rows, :] = d[:, r * HD : (r + 1) * HD]

    @pl.when(place[0] == 1)
    def _():
        for r in range(GROUP):
            h = GROUP + r
            qs[r * rows : (r + 1) * rows, :] = other[:, r * HD : (r + 1) * HD]
            ds[r * rows : (r + 1) * rows, :] = other[:, h * HD : (h + 1) * HD]

    ds[...] = by_parity(ds[...], share)

    def chunk_rows(c):
        return pl.ds(pl.multiple_of(c * CHUNK, CHUNK), CHUNK)

    def clear(c, carry):
        out[chunk_rows(c), :] = jnp.zeros((CHUNK, HD), out.dtype)
        return carry

    lax.fori_loop(high + 1, seq // CHUNK, clear, 0)

    def absorb(x, top, total):
        x = x.reshape(CHUNK // 8, 8, width)
        larger = jnp.maximum(top, jnp.max(x, axis=0))
        total = total * jnp.exp2(top - larger) + jnp.sum(jnp.exp2(x - larger), axis=0)
        return larger, total

    def inner(c, carry):
        x = product(k[chunk_rows(c), :], qs[...], 1) * GAIN
        s[chunk_rows(c), :] = x
        return absorb(x, *carry)

    empty = jnp.full((8, width), masked_score, jnp.float32), jnp.zeros((8, width), jnp.float32)
    top, total = lax.fori_loop(0, high, inner, empty)
    query_pos = first_row + lanes_of_queries(lax.broadcasted_iota(jnp.int32, (1, rows), 1))
    key_pos = high * CHUNK + lax.broadcasted_iota(jnp.int32, (CHUNK, width), 0)
    x = product(k[chunk_rows(high), :], qs[...], 1) * GAIN
    x = jnp.where(key_pos <= query_pos, x, masked_score)
    s[chunk_rows(high), :] = x
    top, total = absorb(x, top, total)
    most = jnp.max(top, axis=0, keepdims=True)
    total = jnp.sum(total * jnp.exp2(top - most), axis=0, keepdims=True)
    shift = most + jnp.log2(total)

    def collect(c, carry):
        p = jnp.exp2(s[chunk_rows(c), :] - shift).astype(ds.dtype)
        block = product(p, ds[...], 0)
        for i in range(0, CHUNK // rows, 2):
            pair = [block[(i + n) * rows : (i + n + 1) * rows] for n in range(2)]
            for parity in range(2):
                at = pl.ds(pl.multiple_of(c * CHUNK + (i + parity) * rows, rows), rows)
                out[at, :] = join(*pair, parity).astype(out.dtype)
        return carry

    lax.fori_loop(0, high + 1, collect, 0)


def value_kernel(pieces, out):
    total = pieces[0].astype(jnp.float32)
    for i in range(1, pieces.shape[0]):
        total = total + pieces[i].astype(jnp.float32)
    out[...] = total.astype(out.dtype)


def project_kernel(
    place, values, stay, got, near, far, mine, across, beside, corner, out, turned, vg
):
    rows = values.shape[1]
    group, core = place[0], place[4]
    half = HD // 2
    for g in range(KV_HEADS):
        part = jnp.transpose(values[g, :, :HD].astype(jnp.float32))
        for c in range(2):
            turned[c, g * half : (g + 1) * half, :] = part[c * half : (c + 1) * half]
    for n, (here, sent) in enumerate(((stay, near), (got, far))):
        part = jnp.where(group == 1, here[...].astype(jnp.float32), sent[...].astype(jnp.float32))
        turned[2 + n] = jnp.transpose(part)
    for j in range(4):
        g = group if j % 2 == 0 else 1 - group
        c = core if j // 2 == 0 else 1 - core
        block = turned[jnp.where(g == 0, c, 2 + j // 2)]
        vg[:, j * rows : (j + 1) * rows] = block.astype(vg.dtype)
    chips, stripes, depth, span = out.shape
    span = span // 2
    for t in range(0, stripes, 2):
        part = slice(t * span, (t + 2) * span)
        x = jnp.concatenate(
            [mine[:, part], across[:, part], beside[:, part], corner[:, part]], axis=0
        )
        block = product(vg[...], x, 0)
        for n in range(2):
            piece = block[:, n * span : (n + 1) * span].reshape(chips, 2, depth, span)
            piece = jnp.concatenate([piece[:, 0], piece[:, 1]], axis=-1)
            out[:, t + n] = piece.astype(out.dtype)


def fold_kernel(owners, pieces, out, total):
    acc = pieces[0].astype(jnp.float32)
    for i in range(1, pieces.shape[0]):
        acc = acc + pieces[i].astype(jnp.float32)
    total[...] = acc
    half = total.shape[1] // 2
    span = half // owners
    out[...] = jnp.zeros(out.shape, out.dtype)
    for r in range(owners):
        out[r, :, :span] = total[:, r * span : (r + 1) * span]
        out[r, :, 64 : 64 + span] = total[:, half + r * span : half + (r + 1) * span]


def adam_kernel(scale, pieces, m, v, new_m, new_v, update):
    acc = pieces[0]
    for i in range(1, pieces.shape[0]):
        acc = acc + pieces[i]
    span = m.shape[1]
    gradient = jnp.concatenate([acc[:, :span], acc[:, 64 : 64 + span]], axis=0) * scale
    first = 0.9 * m[...] + 0.1 * gradient
    second = 0.95 * v[...] + 0.05 * gradient * gradient
    new_m[...] = first
    new_v[...] = second
    update[...] = first / (1.0 - 0.9**STEP) / (jnp.sqrt(second / (1.0 - 0.95**STEP)) + 1e-08)


def call(kernel, out, scalars, arrays, scratch=(), flops=0):
    many = isinstance(out, tuple)
    return pl.pallas_call(
        kernel,
        out_shape=out,
        in_specs=[SCALARS] * len(scalars) + [WHOLE] * len(arrays),
        out_specs=(WHOLE,) * len(out) if many else WHOLE,
        scratch_shapes=list(scratch),
        compiler_params=PARAMS,
        cost_estimate=pl.CostEstimate(flops=flops, bytes_accessed=0, transcendentals=0),
    )(*scalars, *arrays)


def body(layer_input, queries, keys, d_out, doc_start, moment_m, moment_v):
    rows = queries.shape[1]
    chips, cores = lax.axis_size("x"), lax.axis_size("core")
    stripes, owners = lax.axis_size("yh"), lax.axis_size("z")
    blocks = chips * cores
    seq = blocks * rows
    width, cols = layer_input.shape[2], KV_HEADS * HD
    half, share = width // 2, cols // blocks
    heads = GROUP * HD
    bf16, f32 = jnp.bfloat16, jnp.float32
    shape = jax.ShapeDtypeStruct

    group, core = lax.axis_index("grp"), lax.axis_index("core")
    index = lax.axis_index("x") * cores + core
    first_row = index * rows
    place = jnp.stack([group, first_row, first_row // CHUNK, index, core]).astype(jnp.int32)
    q, d, k = queries[0], d_out[0], keys[0]

    down, swap = [(0, 1)], [(0, 1), (1, 0)]
    other_k = lax.ppermute(k, "grp", down)
    other = lax.ppermute(jnp.concatenate([q[:, heads:], d[:, heads:]], axis=1), "grp", down)
    lower, upper = layer_input[0, :, :half], layer_input[0, :, half:]
    mine = jnp.where(group == 0, lower, upper)
    theirs = jnp.where(group == 0, upper, lower)
    across = lax.ppermute(theirs, "grp", swap)
    chosen = jnp.where(group == 0, k[:, :HD], other_k[:, HD:])
    all_keys = lax.all_gather(chosen, ("x", "core"), axis=0).reshape(seq, HD)
    partial = call(
        functools.partial(long_kernel, share),
        shape((seq, HD), bf16),
        [place],
        [q, d, other, all_keys],
        [
            pltpu.VMEM((heads, HD), bf16),
            pltpu.VMEM((heads, HD), bf16),
            pltpu.VMEM((seq, GROUP * rows), f32),
        ],
        flops=6 * 10**9,
    )
    partial, across, mine, begin = lax.optimization_barrier((partial, across, mine, doc_start))
    square = shape((rows, HD), bf16)
    stay, leave = call(
        functools.partial(local_kernel, share),
        (square, square),
        [place],
        [begin, q, d, k],
        [pltpu.VMEM((heads, HD), bf16), pltpu.VMEM((heads, HD), bf16)],
        flops=3 * 10**9,
    )
    beside = lax.ppermute(mine, "core", swap)
    corner = lax.ppermute(across, "core", swap)
    got = lax.ppermute(leave, "core", swap)
    near = lax.ppermute(stay, "grp", [(1, 0)])
    far = lax.ppermute(leave, ("grp", "core"), [(2, 1), (3, 0)])
    pieces = lax.all_to_all(
        partial.reshape(blocks, rows, HD), ("x", "core"), 0, 0, tiled=True
    )
    values = call(value_kernel, square, [], [pieces])
    values = lax.all_gather(values, "grp", axis=0)
    gradient = call(
        project_kernel,
        shape((chips, stripes, share // 2, 2 * half // stripes), bf16),
        [place],
        [values, stay, got, near, far, mine, across, beside, corner],
        [pltpu.VMEM((4, cols // 2, rows), f32), pltpu.VMEM((cols // 2, 4 * rows), bf16)],
    )
    gradient = gradient.reshape(chips * stripes, share // 2, 2 * half // stripes)
    terms = lax.all_to_all(gradient, ("x", "yh"), 0, 0, tiled=True)
    sent = call(
        functools.partial(fold_kernel, owners),
        shape((owners, 8, 128), f32),
        [],
        [terms],
        [pltpu.VMEM((share // 2, 2 * half // stripes), f32)],
    )
    landed = lax.all_to_all(sent, "z", 0, 0, tiled=True)
    result = shape(moment_m.shape[::-1], f32)
    total_tokens = 2 * stripes * owners * seq
    outs = call(
        functools.partial(adam_kernel, 1.0 / math.sqrt(total_tokens)),
        (result,) * 3,
        [],
        [landed, moment_m.T, moment_v.T],
    )
    return tuple(o.T for o in outs)


def solution(mesh):
    groups, copies, blocks = mesh.devices.shape
    split = mesh.devices.reshape(groups, 4, copies // 4, blocks // 2, 2)
    mesh = Mesh(split, ("grp", "yh", "z", "x", "core"))
    slots, tokens = ("grp", "yh", "z"), ("x", "core")
    wide, flat = P(slots, tokens, None), P(slots, tokens)
    in_specs = (wide, wide, wide, wide, flat, flat, flat)
    return jax.shard_map(
        body, mesh=mesh, in_specs=in_specs, out_specs=(flat,) * 3, check_vma=False
    )
```
